128 devices in a mesh: batch: 2 (over z_lo), seq: 32 (over y, x, core), tensor: 2 (over z_hi).
Axes of the slice: x: 4, y: 4, z: 4 (z_hi: 2, z_lo: 2; z = z_hi * 2 + z_lo), core: 2. Of those that a mesh axis runs over, the one named last changes fastest.
Arguments:
- tokens: bfloat16 [8192, 2560], P(('batch', 'seq')), may hold values from -6 to 6
- cotangent: bfloat16 [8192, 2560], P(('batch', 'seq')), may hold values from -6 to 6
- query_weight: float32 [2560, 2560], P(('batch', 'seq'), 'tensor'), may hold values from -0.125 to 0.125
- query_moment: float32 [2560, 2560], P(('batch', 'seq'), 'tensor'), may hold values from -16 to 16
- query_second: float32 [2560, 2560], P(('batch', 'seq'), 'tensor'), may hold values from 26.95168 to 107.80672
- keyvalue_weight: float32 [2560, 512], P(('batch', 'seq')), may hold values from -0.125 to 0.125
- keyvalue_moment: float32 [2560, 512], P(('batch', 'seq')), may hold values from -64 to 64
- keyvalue_second: float32 [2560, 512], P(('batch', 'seq')), may hold values from 430.8992 to 1724.416
- output_weight: float32 [2560, 2560], P(('batch', 'seq'), 'tensor'), may hold values from -0.625 to 0.625
- output_moment: float32 [2560, 2560], P(('batch', 'seq'), 'tensor'), may hold values from -6 to 6
- output_second: float32 [2560, 2560], P(('batch', 'seq'), 'tensor'), may hold values from 17.2032 to 68.8128
- feedforward_weight: float32 [3, 2560, 7680], P(None, ('batch', 'seq'), 'tensor'), may hold values from -0.125 to 0.125
- feedforward_moment: float32 [3, 2560, 7680], P(None, ('batch', 'seq'), 'tensor'), may hold values from -32 to 32
- feedforward_second: float32 [3, 2560, 7680], P(None, ('batch', 'seq'), 'tensor'), may hold values from 107.80672 to 430.8992
- norm_gains: float32 [2, 2560], P(None, ('batch', 'seq')), may hold values from 0.5 to 1.5
- gains_moment: float32 [2, 2560], P(None, ('batch', 'seq')), may hold values from -32 to 32
- gains_second: float32 [2, 2560], P(None, ('batch', 'seq')), may hold values from 107.80672 to 430.8992
Outputs:
- out_tokens: bfloat16 [8192, 2560], P(('batch', 'seq'))
- input_grad: float32 [8192, 2560], P(('batch', 'seq'))
- query_moment_new: float32 [2560, 2560], P(('batch', 'seq'), 'tensor')
- query_second_new: float32 [2560, 2560], P(('batch', 'seq'), 'tensor')
- query_weight_new: float32 [2560, 2560], P(('batch', 'seq'), 'tensor')
- keyvalue_moment_new: float32 [2560, 512], P(('batch', 'seq'))
- keyvalue_second_new: float32 [2560, 512], P(('batch', 'seq'))
- keyvalue_weight_new: float32 [2560, 512], P(('batch', 'seq'))
- output_moment_new: float32 [2560, 2560], P(('batch', 'seq'), 'tensor')
- output_second_new: float32 [2560, 2560], P(('batch', 'seq'), 'tensor')
- output_weight_new: float32 [2560, 2560], P(('batch', 'seq'), 'tensor')
- feedforward_moment_new: float32 [3, 2560, 7680], P(None, ('batch', 'seq'), 'tensor')
- feedforward_second_new: float32 [3, 2560, 7680], P(None, ('batch', 'seq'), 'tensor')
- feedforward_weight_new: float32 [3, 2560, 7680], P(None, ('batch', 'seq'), 'tensor')
- gains_moment_new: float32 [2, 2560], P(None, ('batch', 'seq'))
- gains_second_new: float32 [2, 2560], P(None, ('batch', 'seq'))
- norm_gains_new: float32 [2, 2560], P(None, ('batch', 'seq'))
The draws below stay inside these ranges and needn't reach their ends.
All inputs are finite; a program needn't handle non-finite values.
Results may differ from the reference program's by a relative error of at most 0.018.
Values may be sent and summed in bfloat16 or wider, within the bound.
No kernel may reach another device: no remote copies, remote signals or barrier semaphores. Data moves between devices by JAX's collectives and lax.ppermute only.
A program may use at most 576 MiB of HBM per device.

```python
import math
import jax
import jax.numpy as jnp
from jax import lax

D = 2560
HEADS = 10
HEAD_DIM = 256
FF = 7680
WINDOW = 2048
STEP = 10
LENGTH = 4096
TOKENS = 8192
N_BATCH = 2


def level_of(own_key, extent, pieces, low, top_value):
    def one(axis_at, blocks):
        heights = jax.random.uniform(jax.random.fold_in(jax.random.fold_in(own_key, 6), axis_at), (blocks,), jnp.float32, low / len(pieces), top_value / len(pieces))
        return jnp.repeat(jnp.exp(heights), extent[axis_at] // blocks).reshape((-1,) + (1,) * (len(extent) - axis_at - 1))

    level = one(*pieces[0])
    for cut in pieces[1:]:
        level = level * one(*cut)
    return level


def gaussian(rng, extent, width, most, split=(), kind=jnp.bfloat16):
    level = level_of(rng, extent, split, -0.22, 0.18) if split else 1.0
    array = jax.random.normal(rng, extent, jnp.float32) * width * level
    return jnp.minimum(jnp.maximum(array, -most), most).astype(kind)


def setup_inputs(seed: int = 0) -> dict:
    key_list = jax.random.split(jax.random.key(seed), 18)
    return {
        "tokens": gaussian(key_list[0], (TOKENS, D), 1.0, 6.0, ((0, 64),)),
        "cotangent": gaussian(key_list[1], (TOKENS, D), 1.0, 6.0, ((0, 64),)),
        "query_weight": gaussian(key_list[2], (D, HEADS * HEAD_DIM), D ** -0.5, 0.125, ((0, 64), (1, 2)), jnp.float32),
        "query_moment": gaussian(key_list[3], (D, HEADS * HEAD_DIM), (0.0278 * TOKENS ** 0.5), 16.0, ((0, 64), (1, 2)), jnp.float32),
        "query_second": jnp.clip(jnp.exp(math.log(107.80672) - 1.3862944 * jax.random.uniform(key_list[4], (D, HEADS * HEAD_DIM), jnp.float32) ** level_of(key_list[4], (D, HEADS * HEAD_DIM), ((0, 64), (1, 2)), -0.2, 0.2)), 26.95168, 107.80672),
        "keyvalue_weight": gaussian(key_list[5], (D, 2 * HEAD_DIM), D ** -0.5, 0.125, ((0, 64),), jnp.float32),
        "keyvalue_moment": gaussian(key_list[6], (D, 2 * HEAD_DIM), (0.111 * TOKENS ** 0.5), 64.0, ((0, 64),), jnp.float32),
        "keyvalue_second": jnp.clip(jnp.exp(math.log(1724.416) - 1.3867695 * jax.random.uniform(key_list[7], (D, 2 * HEAD_DIM), jnp.float32) ** level_of(key_list[7], (D, 2 * HEAD_DIM), ((0, 64),), -0.2, 0.2)), 430.8992, 1724.416),
        "output_weight": gaussian(key_list[8], (D, HEADS * HEAD_DIM), (HEADS * HEAD_DIM // 32) ** -0.5, 0.625, ((0, 64), (1, 2)), jnp.float32),
        "output_moment": gaussian(key_list[9], (D, HEADS * HEAD_DIM), (0.0222 * TOKENS ** 0.5), 6.0, ((0, 64), (1, 2)), jnp.float32),
        "output_second": jnp.clip(jnp.exp(math.log(68.8128) - 1.3862944 * jax.random.uniform(key_list[10], (D, HEADS * HEAD_DIM), jnp.float32) ** level_of(key_list[10], (D, HEADS * HEAD_DIM), ((0, 64), (1, 2)), -0.2, 0.2)), 17.2032, 68.8128),
        "feedforward_weight": gaussian(key_list[11], (3, D, FF), D ** -0.5, 0.125, ((1, 64), (2, 2)), jnp.float32),
        "feedforward_moment": gaussian(key_list[12], (3, D, FF), (0.0555 * TOKENS ** 0.5), 32.0, ((1, 64), (2, 2)), jnp.float32),
        "feedforward_second": jnp.clip(jnp.exp(math.log(430.8992) - 1.3855342 * jax.random.uniform(key_list[13], (3, D, FF), jnp.float32) ** level_of(key_list[13], (3, D, FF), ((1, 64), (2, 2)), -0.2, 0.2)), 107.80672, 430.8992),
        "norm_gains": jnp.clip(1.0 + 0.1 * jax.random.normal(key_list[14], (2, D), jnp.float32), 0.5, 1.5),
        "gains_moment": gaussian(key_list[15], (2, D), (0.0555 * TOKENS ** 0.5), 32.0, ((1, 64),), jnp.float32),
        "gains_second": jnp.clip(jnp.exp(math.log(430.8992) - 1.3855342 * jax.random.uniform(key_list[16], (2, D), jnp.float32) ** level_of(key_list[16], (2, D), ((1, 64),), -0.2, 0.2)), 107.80672, 430.8992),
    }


HIGH = lax.Precision.HIGHEST

@jax.custom_vjp
def low(v):
    return lax.optimization_barrier(v.astype(jnp.bfloat16)).astype(jnp.float32)

@jax.custom_vjp
def low_back(v):
    return v

def low_keep(v):
    return (low(v), None)

def low_pass(kept, grad):
    return (grad,)

def back_keep(v):
    return (v, None)

def back_low(kept, grad):
    return (low(grad),)
low.defvjp(low_keep, low_pass)
low_back.defvjp(back_keep, back_low)

def dot_high(left, right):
    return jnp.dot(left, right, precision=HIGH, preferred_element_type=jnp.float32)

def rms_scale(values, gain):
    return values * lax.rsqrt(lax.optimization_barrier(jnp.mean(values * values, axis=-1, keepdims=True)) + 1e-06) * gain

def rotate(values, places, sign):
    half = values.shape[-1] // 2
    steps = jnp.arange(half, dtype=jnp.float32)
    freqs = jnp.exp(steps * (-2.0 * math.log(10000.0) / values.shape[-1]))
    angle = places[:, None] * freqs[None, :]
    cosine = jnp.cos(angle)[:, None, :]
    sine = sign * jnp.sin(angle)[:, None, :]
    first = values[..., :half]
    second = values[..., half:]
    return jnp.concatenate([first * cosine - second * sine, second * cosine + first * sine], axis=-1)

def attend(queries, key_rows, value_rows):
    length = queries.shape[0]
    block_rows = min(512, length)
    key_span = min(length, WINDOW + block_rows)
    scaling = queries.shape[-1] ** (-0.5)

    def one_block(number):
        opening = number * block_rows
        key_start = jnp.clip(opening + block_rows - key_span, 0, length - key_span)
        q_rows = lax.dynamic_slice_in_dim(queries, opening, block_rows, 0)
        k_rows = lax.dynamic_slice_in_dim(key_rows, key_start, key_span, 0)
        v_rows = lax.dynamic_slice_in_dim(value_rows, key_start, key_span, 0)
        scores = low_back(jnp.einsum('qhd,kd->hqk', q_rows, k_rows, precision=HIGH) * scaling)
        distance = (opening + jnp.arange(block_rows, dtype=jnp.int32))[:, None] - (key_start + jnp.arange(key_span, dtype=jnp.int32))[None, :]
        inside = (distance >= 0) & (distance < WINDOW)
        scores = jnp.where(inside[None], scores, -1e+30)
        row_max = lax.optimization_barrier(jnp.max(scores, axis=-1, keepdims=True))
        weights_exp = jnp.exp(scores - row_max)
        probs = low(weights_exp / lax.optimization_barrier(jnp.sum(weights_exp, axis=-1, keepdims=True)))
        return jnp.einsum('hqk,kd->qhd', probs, v_rows, precision=HIGH)
    blocks = lax.map(jax.checkpoint(one_block), jnp.arange(length // block_rows, dtype=jnp.int32))
    return blocks.reshape(length, -1)

def forward(inflow, w_query, w_pair, w_output, w_feed, gain_pair):
    gain_low = low(gain_pair)
    normed_a = low(rms_scale(inflow, gain_low[0]))
    query_raw = low_back(dot_high(normed_a, low(w_query)))
    pair_raw = low_back(dot_high(normed_a, low(w_pair)))
    length = inflow.shape[0]
    places = jnp.arange(length, dtype=jnp.float32)
    queries = low(rotate(query_raw.reshape(length, HEADS, HEAD_DIM), places, 1.0))
    key_rows = low(rotate(pair_raw[:, None, :HEAD_DIM], places, 1.0)[:, 0])
    value_rows = low(pair_raw[:, HEAD_DIM:])
    attended = low(low_back(attend(queries, key_rows, value_rows)))
    branch = low_back(dot_high(attended, low(w_output).T))
    residual = inflow + branch
    normed_b = low(rms_scale(residual, gain_low[1]))
    feed_low = low(w_feed)
    gate_pre = low_back(dot_high(normed_b, feed_low[0]))
    up_pre = low_back(dot_high(normed_b, feed_low[1]))
    activated = low(jax.nn.gelu(gate_pre, approximate=True) * up_pre)
    return residual + dot_high(activated, feed_low[2].T)

def adam(weight, grad, moment, second, rate, decay):
    moment_new = 0.9 * moment + 0.1 * grad
    second_new = 0.95 * second + 0.05 * grad * grad
    ratio = moment_new / (1.0 - 0.9 ** STEP) / (jnp.sqrt(second_new / (1.0 - 0.95 ** STEP)) + 1e-08)
    return (moment_new, second_new, weight - rate * (ratio + decay * weight))

def reference(tokens, cotangent, query_weight, query_moment, query_second, keyvalue_weight, keyvalue_moment, keyvalue_second, output_weight, output_moment, output_second, feedforward_weight, feedforward_moment, feedforward_second, norm_gains, gains_moment, gains_second):
    weights = (query_weight, keyvalue_weight, output_weight, feedforward_weight, norm_gains)
    inflow = tokens.astype(jnp.float32).reshape(N_BATCH, LENGTH, D)
    backflow = cotangent.astype(jnp.float32).reshape(N_BATCH, LENGTH, D)

    def per_sequence(totals, paired):
        seq_in, seq_back = paired
        result, pull = jax.vjp(forward, seq_in, *weights)
        grads = pull(seq_back)
        summed = tuple((total + grad for total, grad in zip(totals, grads[1:])))
        return (summed, (result, grads[0]))
    zeros = tuple((jnp.zeros_like(matrix) for matrix in weights))
    totals, (outflow, in_grads) = lax.scan(per_sequence, zeros, (inflow, backflow))
    wide_rate = 1.5 * D ** (-0.5)
    output_rate = 1.5 * (HEADS * HEAD_DIM // 32) ** (-0.5)
    query_new = adam(query_weight, totals[0], query_moment, query_second, wide_rate, 0.1)
    pair_new = adam(keyvalue_weight, totals[1], keyvalue_moment, keyvalue_second, wide_rate, 0.1)
    output_new = adam(output_weight, totals[2], output_moment, output_second, output_rate, 0.1)
    feed_new = adam(feedforward_weight, totals[3], feedforward_moment, feedforward_second, wide_rate, 0.1)
    gains_new = adam(norm_gains, totals[4], gains_moment, gains_second, 0.3, 0.0)
    return (outflow.reshape(TOKENS, D).astype(jnp.bfloat16), in_grads.reshape(TOKENS, D), query_new[0], query_new[1], query_new[2], pair_new[0], pair_new[1], pair_new[2], output_new[0], output_new[1], output_new[2], feed_new[0], feed_new[1], feed_new[2], gains_new[0], gains_new[1], gains_new[2])
```

```python
import math

import jax
import jax.numpy as jnp
from jax import lax
from jax.experimental import pallas as pl
from jax.experimental.pallas import tpu as pltpu
from jax.sharding import Mesh
from jax.sharding import PartitionSpec as P

D = 2560
HEADS = 10
HEAD_DIM = 256
STEP = 10
ROWS = 128
GROUP = 8
OWNED = 40
Q_PART = 160
KV_PART = 64
F_PART = 480
F_PAD = 512
LOCAL_HEADS = 5
TILES = 17
BF = jnp.bfloat16
F32 = jnp.float32
ANY = pl.BlockSpec(memory_space=pl.ANY)
SMEM = pl.BlockSpec(memory_space=pltpu.SMEM)
VMEM = pl.BlockSpec(memory_space=pltpu.VMEM)


def params(mib):
    return pltpu.CompilerParams(vmem_limit_bytes=mib * 1024 * 1024)


def dot(left, right, left_dim, right_dim):
    return lax.dot_general(
        left, right, (((left_dim,), (right_dim,)), ((), ())), preferred_element_type=F32
    )


def shift(value, axis, step):
    return lax.ppermute(value, axis, [(i, (i + step) % 4) for i in range(4)])


def push(value, axis, step):
    return lax.ppermute(value, axis, [(i, i + step) for i in range(4) if 0 <= i + step < 4])


def swap(value, axis):
    return lax.ppermute(value, axis, [(0, 1), (1, 0)])


def place(pieces, index, shape, target):
    count = len(pieces)

    def body(index_ref, *refs):
        out, sems = refs[count], refs[count + 1]
        copies = [
            pltpu.make_async_copy(refs[k], target(out, index_ref, k), sems.at[k])
            for k in range(count)
        ]
        for copy in copies:
            copy.start()
        for copy in copies:
            copy.wait()

    return pl.pallas_call(
        body,
        out_shape=jax.ShapeDtypeStruct(shape, pieces[0].dtype),
        in_specs=[SMEM] + [VMEM] * count,
        out_specs=ANY,
        scratch_shapes=[pltpu.SemaphoreType.DMA((count,))],
        compiler_params=params(24),
    )(index, *pieces)


def ring_pieces(value, axis):
    half = value.shape[0] // 2
    left = shift(value, axis, 1)
    right = shift(value, axis, -1)
    top = shift(left[:half], axis, 1)
    bottom = shift(right[half:], axis, -1)
    return [value, left, right, top, bottom]


def group_pieces(value):
    mine = ring_pieces(value, "x")
    return mine + [swap(piece, "c") for piece in mine]


RING = ((0, None), (1, None), (2, None), (3, 0), (3, 1))


def group_gather(value, index):
    half = value.shape[0] // 2
    shape = (GROUP, 2, half) + value.shape[1:]
    pieces = []
    for k, piece in enumerate(group_pieces(value)):
        if RING[k % 5][1] is None:
            piece = piece.reshape((2, half) + value.shape[1:])
        pieces.append(piece)

    def target(out, index_ref, k):
        slot, part = RING[k % 5]
        spot = index_ref[slot + 4 * (k // 5)]
        return out.at[spot] if part is None else out.at[spot, part]

    out = place(pieces, index, shape, target)
    return out.reshape((GROUP,) + value.shape)


def row_gather(value, group_index, outer_index):
    width = value.shape[1]
    pair = jnp.stack([value, swap(value, "b")])
    pieces = ring_pieces(pair, "y")

    def outer_target(out, index_ref, k):
        slot, part = RING[k]
        spot = index_ref[slot]
        return out.at[spot] if part is None else out.at[spot, part]

    by_y = place(
        [p if RING[k][1] is None else p.reshape(OWNED, width) for k, p in enumerate(pieces)],
        outer_index,
        (4, 2, OWNED, width),
        outer_target,
    )
    block = by_y.transpose(1, 0, 2, 3).reshape(8, OWNED, width)
    first = lax.axis_index("b") * 4
    block = jnp.roll(block, first, axis=0)
    half = 4

    def target(out, index_ref, k):
        slot, part = RING[k % 5]
        spot = index_ref[slot + 4 * (k // 5)]
        if part is None:
            return out.at[:, spot]
        return out.at[pl.ds(part * half, half), spot]

    out = place(group_pieces(block), group_index, (8, GROUP, OWNED, width), target)
    return out.reshape(D, width)


def group_scatter(parts, x, c):
    low = lax.optimization_barrier(parts.astype(BF))
    shaped = low.reshape((4, 2) + low.shape[1:])
    theirs = lax.dynamic_index_in_dim(shaped, 1 - c, 1, keepdims=False)
    mine = lax.dynamic_index_in_dim(shaped, c, 1, keepdims=False)
    both = mine.astype(F32) + swap(theirs, "c").astype(F32)
    half = both.shape[1] // 2

    def block(step):
        return lax.dynamic_index_in_dim(both, (x + step) % 4, 0, keepdims=False)

    own, left, right, far = block(0), block(3), block(1), block(2)
    far_top = shift(far[:half].astype(BF), "x", -1)
    far_bottom = shift(far[half:].astype(BF), "x", 1)
    left_bottom = shift(left[half:].astype(BF), "x", -1)
    right_top = shift(right[:half].astype(BF), "x", 1)
    left_top = shift((left[:half] + far_top.astype(F32)).astype(BF), "x", -1)
    right_bottom = shift((right[half:] + far_bottom.astype(F32)).astype(BF), "x", 1)
    top = own[:half] + left_top.astype(F32) + right_top.astype(F32)
    bottom = own[half:] + left_bottom.astype(F32) + right_bottom.astype(F32)
    return jnp.concatenate([top, bottom], axis=0)


def tensor_sum(value):
    low = lax.optimization_barrier(value.astype(BF))
    return low.astype(F32) + swap(low, "t").astype(F32)


def exchange(value):
    return lax.all_to_all(value, ("x", "c"), split_axis=0, concat_axis=0, tiled=True)


def pack_small(q_ref, kv_ref, gain_ref, out_ref):
    rest = jnp.zeros((OWNED, 256 - Q_PART - KV_PART - 2), F32)
    for j in range(GROUP):
        out_ref[j] = jnp.concatenate(
            [
                q_ref[:, Q_PART * j : Q_PART * (j + 1)],
                kv_ref[:, KV_PART * j : KV_PART * (j + 1)],
                gain_ref[...],
                rest,
            ],
            axis=1,
        ).astype(BF)


def pack_feed(w_ref, out_ref):
    rest = jnp.zeros((OWNED, F_PAD - F_PART), F32)
    for j in range(GROUP):
        out_ref[j] = jnp.concatenate(
            [w_ref[0, :, F_PART * j : F_PART * (j + 1)], rest], axis=1
        ).astype(BF)


def adam(weight, grad, moment, second, rate, decay):
    moment_new = 0.9 * moment + 0.1 * grad
    second_new = 0.95 * second + 0.05 * grad * grad
    ratio = moment_new / (1.0 - 0.9**STEP) / (jnp.sqrt(second_new / (1.0 - 0.95**STEP)) + 1e-08)
    return (moment_new, second_new, weight - rate * (ratio + decay * weight))


def adam_columns(part, start, rate):
    def body(g_ref, w_ref, m_ref, v_ref, mo_ref, vo_ref, wo_ref):
        grad = jnp.concatenate(
            [g_ref[j, :, start : start + part].astype(F32) for j in range(GROUP)], axis=1
        )
        index = (0,) if len(w_ref.shape) == 3 else (slice(None),)
        m, v, w = adam(w_ref[index], grad, m_ref[index], v_ref[index], rate, 0.1)
        mo_ref[index] = m
        vo_ref[index] = v
        wo_ref[index] = w

    return body


def attend_place(base_ref, i):
    block = base_ref[0] * 8 + base_ref[1] + (i - 16 + 32)
    return block % 8, base_ref[0] + 4 - block // 8, block >= 32


def attend(base_ref, q_ref, kv_ref, p_ref, a_ref, qs):
    for h in range(LOCAL_HEADS):
        qs[:, ROWS * h : ROWS * (h + 1)] = q_ref[h]
    width = LOCAL_HEADS * ROWS
    key_at = lax.broadcasted_iota(jnp.int32, (ROWS, width), 0)
    query_at = lax.broadcasted_iota(jnp.int32, (ROWS, width), 1) % ROWS
    top = jnp.full((1, width), -1e30, F32)
    for i in range(TILES):
        at, back, exists = attend_place(base_ref, i)
        scores = dot(kv_ref[at, back, :HEAD_DIM, :], qs[...], 0, 0) * (HEAD_DIM**-0.5)
        if i == 0:
            scores = jnp.where((key_at > query_at) & exists, scores, -1e30)
        elif i == TILES - 1:
            scores = jnp.where(key_at <= query_at, scores, -1e30)
        else:
            scores = jnp.where(exists, scores, -1e30)
        p_ref[i] = scores
        top = jnp.maximum(top, jnp.max(scores, axis=0, keepdims=True))
    total = jnp.zeros((1, width), F32)
    for i in range(TILES):
        weights = jnp.exp(p_ref[i] - top)
        p_ref[i] = weights
        total = total + jnp.sum(weights, axis=0, keepdims=True)
    scale = 1.0 / total
    result = jnp.zeros((HEAD_DIM, width), F32)
    for i in range(TILES):
        at, back, _ = attend_place(base_ref, i)
        probs = p_ref[i] * scale
        p_ref[i] = probs
        result = result + dot(kv_ref[at, back, HEAD_DIM:, :], probs.astype(BF), 1, 0)
    for h in range(LOCAL_HEADS):
        a_ref[h] = result[:, ROWS * h : ROWS * (h + 1)].astype(BF)


def attend_back(base_ref, q_ref, kv_ref, p_ref, da_ref, dq_ref, dkv_ref, qs, das, dps):
    width = LOCAL_HEADS * ROWS
    for h in range(LOCAL_HEADS):
        qs[:, ROWS * h : ROWS * (h + 1)] = q_ref[h]
        das[:, ROWS * h : ROWS * (h + 1)] = da_ref[h]
    dkv_ref[...] = jnp.zeros(dkv_ref.shape, BF)
    delta = jnp.zeros((1, width), F32)
    for i in range(TILES):
        at, back, _ = attend_place(base_ref, i)
        probs = p_ref[i]
        d_probs = dot(kv_ref[at, back, HEAD_DIM:, :], das[...], 0, 0)
        dps[i] = d_probs
        delta = delta + jnp.sum(probs * d_probs, axis=0, keepdims=True)
        dkv_ref[at, back, HEAD_DIM:, :] = dot(das[...], probs.astype(BF), 1, 1).astype(BF)
    dq = jnp.zeros((HEAD_DIM, width), F32)
    for i in range(TILES):
        at, back, _ = attend_place(base_ref, i)
        d_scores = (p_ref[i] * (dps[i] - delta)).astype(BF)
        dq = dq + dot(kv_ref[at, back, :HEAD_DIM, :], d_scores, 1, 0)
        dk = dot(qs[...], d_scores, 1, 1) * (HEAD_DIM**-0.5)
        dkv_ref[at, back, :HEAD_DIM, :] = dk.astype(BF)
    for h in range(LOCAL_HEADS):
        dq_ref[h] = dq[:, ROWS * h : ROWS * (h + 1)] * (HEAD_DIM**-0.5)


def rms_rate(values):
    return lax.rsqrt(jnp.mean(values * values, axis=-1, keepdims=True) + 1e-06)


def rotate(values, cosine, sine):
    first, second = values[..., 0, :, :], values[..., 1, :, :]
    return jnp.stack([first * cosine - second * sine, second * cosine + first * sine], axis=-3)


def local(
    tokens,
    cotangent,
    query_weight,
    query_moment,
    query_second,
    keyvalue_weight,
    keyvalue_moment,
    keyvalue_second,
    output_weight,
    output_moment,
    output_second,
    feedforward_weight,
    feedforward_moment,
    feedforward_second,
    norm_gains,
    gains_moment,
    gains_second,
):
    x, y, c = lax.axis_index("x"), lax.axis_index("y"), lax.axis_index("c")
    j = 2 * x + c
    wide_rate = 1.5 * D**-0.5
    output_rate = 1.5 * (HEADS * HEAD_DIM // 32) ** -0.5
    ring_x = jnp.stack([x, (x + 3) % 4, (x + 1) % 4, (x + 2) % 4]).astype(jnp.int32)
    group_index = jnp.concatenate([2 * ring_x + c, 2 * ring_x + 1 - c])
    outer_index = jnp.stack([y, (y + 3) % 4, (y + 1) % 4, (y + 2) % 4]).astype(jnp.int32)
    base = jnp.stack([y, j]).astype(jnp.int32)

    small = pl.pallas_call(
        pack_small,
        out_shape=jax.ShapeDtypeStruct((GROUP, OWNED, 256), BF),
        in_specs=[VMEM] * 3,
        out_specs=VMEM,
    )(query_weight, keyvalue_weight, norm_gains.T)
    feed = pl.pallas_call(
        pack_feed,
        grid=(3,),
        out_shape=jax.ShapeDtypeStruct((GROUP, OWNED, 3 * F_PAD), BF),
        in_specs=[pl.BlockSpec((1, OWNED, 8 * F_PART), lambda k: (k, 0, 0))],
        out_specs=pl.BlockSpec((GROUP, OWNED, F_PAD), lambda k: (0, 0, k)),
    )(feedforward_weight)
    small = exchange(small).reshape(GROUP * OWNED, 256)
    w_small = lax.all_gather(small, ("b", "y"), axis=0, tiled=True)
    feed = exchange(feed).reshape(GROUP * OWNED, 3 * F_PAD)
    w_feed = lax.all_gather(feed, ("b", "y"), axis=0, tiled=True)
    w_output = row_gather(output_weight.astype(BF), group_index, outer_index)
    w_back = row_gather(
        jnp.concatenate([query_weight, keyvalue_weight], axis=1).astype(BF),
        group_index,
        outer_index,
    )
    gains = w_small[:, Q_PART + KV_PART : Q_PART + KV_PART + 2].astype(F32).T

    inflow = tokens.astype(F32)
    group_tokens = group_gather(tokens, group_index)
    group_flow = group_tokens.astype(F32)
    normed_a = (group_flow * rms_rate(group_flow) * gains[0]).astype(BF).reshape(1024, D)
    raw = dot(w_small, normed_a, 0, 1).astype(BF)
    raw = exchange(raw.reshape(256, GROUP, ROWS).transpose(1, 0, 2))
    steps = jnp.arange(HEAD_DIM // 2, dtype=F32)
    freqs = jnp.exp(steps * (-2.0 * math.log(10000.0) / HEAD_DIM))
    places = ((y * GROUP + j) * ROWS + jnp.arange(ROWS, dtype=jnp.int32)).astype(F32)
    angle = freqs[:, None] * places[None, :]
    cosine, sine = jnp.cos(angle), jnp.sin(angle)
    q_raw = raw[:, :Q_PART].astype(F32).reshape(LOCAL_HEADS, 2, HEAD_DIM // 2, ROWS)
    kv_raw = raw[:, Q_PART : Q_PART + KV_PART].astype(F32).reshape(2, 2, HEAD_DIM // 2, ROWS)
    queries = rotate(q_raw, cosine, sine).astype(BF).reshape(LOCAL_HEADS, HEAD_DIM, ROWS)
    keys = rotate(kv_raw[0], cosine, sine)
    pair = jnp.stack([keys, kv_raw[1]]).astype(BF).reshape(2 * HEAD_DIM, ROWS)
    spans = jnp.concatenate([pair, push(pair, "y", 1), push(pair, "y", 2)])
    spans = group_gather(spans, group_index).reshape(GROUP, 3, 2 * HEAD_DIM, ROWS)

    width = LOCAL_HEADS * ROWS
    probs, attended = pl.pallas_call(
        attend,
        out_shape=(
            jax.ShapeDtypeStruct((TILES, ROWS, width), F32),
            jax.ShapeDtypeStruct((LOCAL_HEADS, HEAD_DIM, ROWS), BF),
        ),
        in_specs=[SMEM, VMEM, VMEM],
        out_specs=(VMEM, VMEM),
        scratch_shapes=[pltpu.VMEM((HEAD_DIM, width), BF)],
        compiler_params=params(40),
    )(base, queries, spans)
    attended = attended.reshape(LOCAL_HEADS * HEAD_DIM, ROWS)
    residual = inflow + tensor_sum(dot(attended, w_output, 0, 1))

    rate_b = rms_rate(residual)
    normed_b = (residual * rate_b * gains[1]).astype(BF)
    group_b = group_gather(normed_b, group_index).reshape(1024, D)
    group_back = group_gather(cotangent, group_index).reshape(1024, D)
    gate_up = dot(group_b, w_feed[:, : 2 * F_PAD], 1, 0)
    gate, up = gate_up[:, :F_PAD], gate_up[:, F_PAD:]
    d_hidden = dot(group_back, w_feed[:, 2 * F_PAD :], 1, 0)
    root = math.sqrt(2.0 / math.pi)
    bend = jnp.tanh(root * (gate + 0.044715 * gate * gate * gate))
    gelu = 0.5 * gate * (1.0 + bend)
    slope = 0.5 * (1.0 + bend) + 0.5 * gate * (1.0 - bend * bend) * root * (
        1.0 + 3.0 * 0.044715 * gate * gate
    )
    hidden = (gelu * up).astype(BF)
    d_gate_up = jnp.concatenate(
        [(d_hidden * up * slope).astype(BF), (d_hidden * gelu).astype(BF)], axis=1
    )
    normb_part = dot(d_gate_up, w_feed[:, : 2 * F_PAD], 1, 1)
    grad_normb = tensor_sum(group_scatter(normb_part.reshape(GROUP, ROWS, D), x, c))
    feed_part = dot(hidden, w_feed[:, 2 * F_PAD :], 1, 1)
    out_sum = tensor_sum(group_scatter(feed_part.reshape(GROUP, ROWS, D), x, c))
    out_tokens = (residual + out_sum).astype(BF)
    down_grad = dot(group_back, hidden, 0, 0).astype(BF)
    gate_grad = dot(group_b, d_gate_up, 0, 0).astype(BF)
    down_grad = lax.psum_scatter(down_grad, ("b", "y"), scatter_dimension=0, tiled=True)
    gate_grad = lax.psum_scatter(gate_grad, ("b", "y"), scatter_dimension=0, tiled=True)

    scaled = grad_normb * gains[1]
    grad_resid = (
        cotangent.astype(F32)
        + rate_b * scaled
        - residual * rate_b**3 * jnp.mean(scaled * residual, axis=-1, keepdims=True)
    )
    gain_b = jnp.sum(grad_normb * residual * rate_b, axis=0)
    resid_low = grad_resid.astype(BF)
    grad_att = dot(w_output, resid_low, 0, 1).astype(BF).reshape(LOCAL_HEADS, HEAD_DIM, ROWS)

    grad_q, grad_spans = pl.pallas_call(
        attend_back,
        out_shape=(
            jax.ShapeDtypeStruct((LOCAL_HEADS, HEAD_DIM, ROWS), F32),
            jax.ShapeDtypeStruct((GROUP, 3, 2 * HEAD_DIM, ROWS), BF),
        ),
        in_specs=[SMEM, VMEM, VMEM, VMEM, VMEM],
        out_specs=(VMEM, VMEM),
        scratch_shapes=[
            pltpu.VMEM((HEAD_DIM, width), BF),
            pltpu.VMEM((HEAD_DIM, width), BF),
            pltpu.VMEM((TILES, ROWS, width), F32),
        ],
        compiler_params=params(44),
    )(base, queries, spans, probs, grad_att)
    back = group_scatter(grad_spans.reshape(GROUP, 3 * 2 * HEAD_DIM, ROWS), x, c)
    back = back.reshape(3, 2 * HEAD_DIM, ROWS)
    back = (
        back[0]
        + push(back[1].astype(BF), "y", -1).astype(F32)
        + push(back[2].astype(BF), "y", -2).astype(F32)
    )
    back = tensor_sum(back).reshape(2, 2, HEAD_DIM // 2, ROWS)
    pair_grad = (
        jnp.stack([rotate(back[0], cosine, -sine), back[1]]).astype(BF).reshape(2 * HEAD_DIM, ROWS)
    )
    query_grad = (
        rotate(grad_q.reshape(LOCAL_HEADS, 2, HEAD_DIM // 2, ROWS), cosine, -sine)
        .astype(BF)
        .reshape(LOCAL_HEADS * HEAD_DIM, ROWS)
    )

    all_grad = jnp.concatenate([query_grad, pair_grad * jnp.asarray(0.5, BF)])
    norma_part = dot(all_grad, w_back, 0, 1)
    rate_a = rms_rate(inflow)
    gain_a = jnp.sum(norma_part * inflow * rate_a, axis=0)
    grad_norma = tensor_sum(norma_part)
    scaled = grad_norma * gains[0]
    input_grad = (
        grad_resid
        + rate_a * scaled
        - inflow * rate_a**3 * jnp.mean(scaled * inflow, axis=-1, keepdims=True)
    )

    sent = jnp.concatenate(
        [query_grad.reshape(GROUP, Q_PART, ROWS), pair_grad.reshape(GROUP, KV_PART, ROWS)], axis=1
    )
    sent = exchange(sent).transpose(1, 0, 2).reshape(Q_PART + KV_PART, 1024)
    small_grad = dot(normed_a, sent, 0, 1)
    gain_terms = jnp.stack([gain_a, 0.5 * gain_b], axis=1)
    small_grad = jnp.concatenate(
        [small_grad, gain_terms, jnp.zeros((D, 256 - Q_PART - KV_PART - 2), F32)], axis=1
    ).astype(BF)
    small_grad = lax.psum_scatter(small_grad, ("b", "y"), scatter_dimension=0, tiled=True)
    small_grad = exchange(small_grad.reshape(GROUP, OWNED, 256))
    sent = exchange(attended.reshape(GROUP, Q_PART, ROWS)).transpose(1, 0, 2)
    group_resid = group_gather(resid_low, group_index).reshape(1024, D)
    output_grad = dot(group_resid, sent.reshape(Q_PART, 1024), 0, 1).astype(BF)
    output_grad = lax.psum_scatter(output_grad, ("b", "y"), scatter_dimension=0, tiled=True)
    output_grad = exchange(output_grad.reshape(GROUP, OWNED, Q_PART))
    down_grad = exchange(down_grad.reshape(GROUP, OWNED, F_PAD))
    gate_grad = exchange(gate_grad.reshape(GROUP, OWNED, 2 * F_PAD))

    def update(grad, weight, moment, second, part, start, rate):
        return pl.pallas_call(
            adam_columns(part, start, rate),
            out_shape=(jax.ShapeDtypeStruct(weight.shape, F32),) * 3,
            in_specs=[VMEM] * 4,
            out_specs=(VMEM,) * 3,
            compiler_params=params(32),
        )(grad, weight, moment, second)

    query_new = update(small_grad, query_weight, query_moment, query_second, Q_PART, 0, wide_rate)
    pair_new = update(
        small_grad, keyvalue_weight, keyvalue_moment, keyvalue_second, KV_PART, Q_PART, wide_rate
    )
    output_new = update(
        output_grad, output_weight, output_moment, output_second, Q_PART, 0, output_rate
    )
    feed_grad = jnp.concatenate([gate_grad, down_grad], axis=2)
    matrix = pl.BlockSpec((1, OWNED, 8 * F_PART), lambda k: (k, 0, 0))
    feed_new = pl.pallas_call(
        adam_columns(F_PART, 0, wide_rate),
        grid=(3,),
        out_shape=(jax.ShapeDtypeStruct(feedforward_weight.shape, F32),) * 3,
        in_specs=[pl.BlockSpec((GROUP, OWNED, F_PAD), lambda k: (0, 0, k))] + [matrix] * 3,
        out_specs=(matrix,) * 3,
        compiler_params=params(32),
    )(feed_grad, feedforward_weight, feedforward_moment, feedforward_second)
    gain_grad = jnp.sum(
        small_grad[:, :, Q_PART + KV_PART : Q_PART + KV_PART + 2].astype(F32), axis=0
    ).T
    gain_grad = gain_grad + swap(gain_grad, "t")
    gains_new = adam(norm_gains, gain_grad, gains_moment, gains_second, 0.3, 0.0)
    return (
        out_tokens,
        input_grad,
        *query_new,
        *pair_new,
        *output_new,
        *feed_new,
        *gains_new,
    )


def solution(mesh):
    grid = Mesh(mesh.devices.reshape(2, 4, 4, 2, 2), ("b", "y", "x", "c", "t"))
    rows = ("b", "y", "x", "c")
    token = P(rows, None)
    split = P(rows, "t")
    whole = P(rows, None)
    feed = P(None, rows, "t")
    gain = P(None, rows)
    weights = (split,) * 3 + (whole,) * 3 + (split,) * 3 + (feed,) * 3 + (gain,) * 3
    return jax.shard_map(
        local,
        mesh=grid,
        in_specs=(token, token) + weights,
        out_specs=(token, token) + weights,
        check_vma=False,
    )
```

```python
import math

import jax
import jax.numpy as jnp
from jax import lax
from jax.experimental import pallas as pl
from jax.experimental.pallas import tpu as pltpu
from jax.sharding import Mesh
from jax.sharding import PartitionSpec as P

D = 2560
HEADS = 10
HEAD_DIM = 256
STEP = 10
ROWS = 128
GROUP = 8
OWNED = 40
Q_PART = 160
KV_PART = 64
F_PART = 480
F_PAD = 512
LOCAL_HEADS = 5
TILES = 17
BF = jnp.bfloat16
F32 = jnp.float32
ANY = pl.BlockSpec(memory_space=pl.ANY)
SMEM = pl.BlockSpec(memory_space=pltpu.SMEM)
VMEM = pl.BlockSpec(memory_space=pltpu.VMEM)


SMALL = pl.CostEstimate(flops=1, transcendentals=0, bytes_accessed=1)


def params(mib):
    return pltpu.CompilerParams(vmem_limit_bytes=mib * 1024 * 1024)


def dot(left, right, left_dim, right_dim):
    return lax.dot_general(
        left, right, (((left_dim,), (right_dim,)), ((), ())), preferred_element_type=F32
    )


def shift(value, axis, step):
    return lax.ppermute(value, axis, [(i, (i + step) % 4) for i in range(4)])


def push(value, axis, step):
    return lax.ppermute(value, axis, [(i, i + step) for i in range(4) if 0 <= i + step < 4])


def swap(value, axis):
    return lax.ppermute(value, axis, [(0, 1), (1, 0)])


STEPS = (0, 1, 3, 2)
Y_AT, X_AT, B_AT, C_AT = 0, 4, 8, 10


def tie(value, *others):
    def body(*refs):
        del refs

    return pl.pallas_call(
        body,
        out_shape=jax.ShapeDtypeStruct(value.shape, value.dtype),
        in_specs=[ANY] * (1 + len(others)),
        out_specs=ANY,
        input_output_aliases={0: 0},
        cost_estimate=SMALL,
    )(value, *others)


def place(pieces, index, shape, target):
    count = len(pieces)

    def body(index_ref, *refs):
        out, sems = refs[count], refs[count + 1]
        copies = [
            pltpu.make_async_copy(refs[k], target(out, index_ref, k), sems.at[k])
            for k in range(count)
        ]
        for copy in copies:
            copy.start()
        for copy in copies:
            copy.wait()

    return pl.pallas_call(
        body,
        out_shape=jax.ShapeDtypeStruct(shape, pieces[0].dtype),
        in_specs=[SMEM] + [VMEM] * count,
        out_specs=ANY,
        scratch_shapes=[pltpu.SemaphoreType.DMA((count,))],
        cost_estimate=SMALL,
        compiler_params=params(24),
    )(index, *pieces)


def direct(value, axis):
    return [value] + [shift(value, axis, step) for step in STEPS[1:]]


def group_place(mine, index):
    pieces = mine + [swap(piece, "c") for piece in mine]

    def target(out, index_ref, k):
        return out.at[2 * index_ref[X_AT + k % 4] + index_ref[C_AT + k // 4]]

    return place(pieces, index, (GROUP,) + mine[0].shape, target)


def group_gather(value, index):
    return group_place(direct(value, "x"), index)


def two_step_gather(value, index):
    half = value.shape[0] // 2
    left, right = shift(value, "x", 1), shift(value, "x", 3)
    top, bottom = shift(left[:half], "x", 1), shift(right[half:], "x", 3)
    mine = [value, left, right, top, bottom]
    pieces = mine + [swap(piece, "c") for piece in mine]
    pieces = [
        piece if k % 5 > 2 else piece.reshape((2, half) + value.shape[1:])
        for k, piece in enumerate(pieces)
    ]

    def target(out, index_ref, k):
        spot = 2 * index_ref[X_AT + min(k % 5, 3)] + index_ref[C_AT + k // 5]
        return out.at[spot] if k % 5 < 3 else out.at[spot, k % 5 - 3]

    out = place(pieces, index, (GROUP, 2, half) + value.shape[1:], target)
    return out.reshape((GROUP,) + value.shape), (left, right)


def place_rows(mine, index):
    pieces = mine + [swap(piece, "c") for piece in mine]

    def target(out, index_ref, k):
        spot = 2 * index_ref[X_AT + min(k % 5, 3)] + index_ref[C_AT + k // 5]
        if k % 5 < 3:
            return out.at[:, spot]
        return out.at[pl.ds((k % 5 - 3) * 4, 4), spot]

    width = mine[0].shape[2]
    return place(pieces, index, (8, GROUP, OWNED, width), target).reshape(D, width)


def pair_gather(mine, theirs, pair_axis, ring_axis, index, after=()):
    pieces = direct(jnp.stack([mine, theirs]), ring_axis)
    ring_at, pair_at = (X_AT, C_AT) if ring_axis == "x" else (Y_AT, B_AT)

    def body(index_ref, *refs):
        out, sems = refs[-2:]
        copies = []
        for k in range(4):
            for h in range(2):
                spot, side = index_ref[ring_at + k], index_ref[pair_at + h]
                to = out.at[spot, side] if ring_axis == "x" else out.at[side, spot]
                copies.append(pltpu.make_async_copy(refs[k].at[h], to, sems.at[2 * k + h]))
        for copy in copies:
            copy.start()
        for copy in copies:
            copy.wait()

    shape = ((4, 2) if ring_axis == "x" else (2, 4)) + mine.shape
    return pl.pallas_call(
        body,
        out_shape=jax.ShapeDtypeStruct(shape, mine.dtype),
        in_specs=[SMEM] + [VMEM] * 4 + [ANY] * len(after),
        out_specs=ANY,
        scratch_shapes=[pltpu.SemaphoreType.DMA((8,))],
        cost_estimate=SMALL,
        compiler_params=params(16),
    )(index, *pieces, *after)


def exchange_sends(mine, theirs, after=()):
    pair = jnp.stack([mine, swap(theirs, "c")], axis=1)
    if after:
        pair = tie(pair, *after)
    return [pair[0]] + [shift(pair[k], "x", STEPS[k]) for k in range(1, 4)]


def exchange_place(pieces, index):
    def body(index_ref, *refs):
        out, sems = refs[-2:]
        copies = []
        for k in range(4):
            for h in range(2):
                to = out.at[index_ref[X_AT + k], index_ref[C_AT + h]]
                copies.append(pltpu.make_async_copy(refs[k].at[h], to, sems.at[2 * k + h]))
        for copy in copies:
            copy.start()
        for copy in copies:
            copy.wait()

    return pl.pallas_call(
        body,
        out_shape=jax.ShapeDtypeStruct((4, 2) + pieces[0].shape[1:], pieces[0].dtype),
        in_specs=[SMEM] + [VMEM] * 4,
        out_specs=ANY,
        scratch_shapes=[pltpu.SemaphoreType.DMA((8,))],
        cost_estimate=SMALL,
        compiler_params=params(16),
    )(index, *pieces)


def group_exchange(mine, theirs, index):
    return exchange_place(exchange_sends(mine, theirs), index)


def fold(mine, received, index, at, after=()):
    shape = mine.shape[1:]

    def body(index_ref, mine_ref, received_ref, *refs):
        for k, out in enumerate(refs[len(after) :]):
            spot = index_ref[at + (0, 2, 1, 3)[k]]
            total = mine_ref[spot].astype(F32) + received_ref[spot].astype(F32)
            out[...] = total.astype(out.dtype)

    return pl.pallas_call(
        body,
        out_shape=(jax.ShapeDtypeStruct(shape, F32),) + (jax.ShapeDtypeStruct(shape, BF),) * 3,
        in_specs=[SMEM, VMEM, VMEM] + [ANY] * len(after),
        out_specs=(VMEM,) * 4,
        cost_estimate=SMALL,
        compiler_params=params(40),
    )(index, mine, received, *after)


def scatter_terms(mine, theirs, pair_axis, ring_axis, index, after=()):
    at = X_AT if ring_axis == "x" else Y_AT
    own, *others = fold(mine, swap(theirs, pair_axis), index, at, after)
    return [own] + [shift(other, ring_axis, step) for step, other in zip(STEPS[1:], others)]


def total_of(terms):
    return sum(term.astype(F32) for term in terms)


def scatter(*args, **kwargs):
    return total_of(scatter_terms(*args, **kwargs))


def pair_total(parts, axis, place_at, pair_axis):
    mine, theirs = sides(parts, axis, place_at)
    return mine.astype(F32) + swap(theirs, pair_axis).astype(F32)


def sides(parts, axis, place_at):
    return (
        lax.dynamic_index_in_dim(parts, place_at, axis, keepdims=False),
        lax.dynamic_index_in_dim(parts, 1 - place_at, axis, keepdims=False),
    )


def both_in_order(mine, theirs, place_at):
    first = place_at == 0
    return jnp.stack([jnp.where(first, mine, theirs), jnp.where(first, theirs, mine)])


def low_bits(value):
    return lax.optimization_barrier(value.astype(BF))


def tensor_sum(low):
    return low.astype(F32) + swap(low, "t").astype(F32)


def exchange(value):
    return lax.all_to_all(value, ("x", "c"), split_axis=0, concat_axis=0, tiled=True)


def hand_out(index_ref, held, mine_ref, theirs_ref):
    for k in range(4):
        spot = 2 * index_ref[X_AT + (0, 2, 1, 3)[k]]
        mine_ref[k] = held[spot + index_ref[C_AT]]
        theirs_ref[k] = held[spot + index_ref[C_AT + 1]]


def pack_small(index_ref, q_ref, kv_ref, gain_ref, mine_ref, theirs_ref, held):
    rest = jnp.zeros((OWNED, 256 - Q_PART - KV_PART - 2), F32)
    half, part = HEAD_DIM // 2, KV_PART // 4
    for j in range(GROUP):
        held[j] = jnp.concatenate(
            [
                q_ref[:, Q_PART * j : Q_PART * (j + 1)],
                kv_ref[:, part * j : part * (j + 1)],
                kv_ref[:, half + part * j : half + part * (j + 1)],
                kv_ref[:, 2 * half + 2 * part * j : 2 * half + 2 * part * (j + 1)],
                gain_ref[...],
                rest,
            ],
            axis=1,
        ).astype(BF)
    hand_out(index_ref, held, mine_ref, theirs_ref)


def pack_feed(index_ref, w_ref, after_ref, mine_ref, theirs_ref, held):
    del after_ref
    rest = jnp.zeros((OWNED, F_PAD - F_PART), F32)
    for j in range(GROUP):
        held[j] = jnp.concatenate(
            [w_ref[0, :, F_PART * j : F_PART * (j + 1)], rest], axis=1
        ).astype(BF)
    hand_out(index_ref, held, mine_ref, theirs_ref)


def adam(weight, grad, moment, second, rate, decay):
    moment_new = 0.9 * moment + 0.1 * grad
    second_new = 0.95 * second + 0.05 * grad * grad
    ratio = moment_new / (1.0 - 0.9**STEP) / (jnp.sqrt(second_new / (1.0 - 0.95**STEP)) + 1e-08)
    return (moment_new, second_new, weight - rate * (ratio + decay * weight))


def adam_columns(part, start, rate, pair=False):
    if pair:
        cuts = [(start, PART), (start + PART, PART), (start + 2 * PART, 2 * PART)]
    else:
        cuts = [(start, part)]

    def body(*refs):
        *g_refs, w_ref, m_ref, v_ref, mo_ref, vo_ref, wo_ref = refs
        grad = sum(
            jnp.concatenate(
                [
                    g_ref[j, :, at : at + count].astype(F32)
                    for at, count in cuts
                    for j in range(GROUP)
                ],
                axis=1,
            )
            for g_ref in g_refs
        )
        index = (0,) if len(w_ref.shape) == 3 else (slice(None),)
        m, v, w = adam(w_ref[index], grad, m_ref[index], v_ref[index], rate, 0.1)
        mo_ref[index] = m
        vo_ref[index] = v
        wo_ref[index] = w

    return body


def window(base_ref, i):
    start = pl.multiple_of(ROWS * (base_ref[1] + i), ROWS)
    return pl.ds(start, ROWS), base_ref[0] * 8 + base_ref[1] + i >= 16


PART = HEAD_DIM // 16


def head_rows(j):
    return (
        (slice(2 * PART * j, 2 * PART * j + PART), slice(PART * j, PART * j + PART)),
        (
            slice(2 * PART * j + PART, 2 * PART * (j + 1)),
            slice(HEAD_DIM // 2 + PART * j, HEAD_DIM // 2 + PART * (j + 1)),
        ),
    )


def hold_spans(index_ref, pieces, keys, values):
    for k, piece in enumerate(pieces):
        spot = 2 * index_ref[X_AT + k % 4] + index_ref[C_AT + k // 4]
        rows = pl.ds(pl.multiple_of(2 * PART * spot, 2 * PART), 2 * PART)
        for back in range(3):
            lanes = slice(1024 * (2 - back), 1024 * (3 - back))
            keys[rows, lanes] = piece[back, : 2 * PART]
            values[rows, lanes] = piece[back, 2 * PART :]


def hold_queries(q_ref, qs):
    for h in range(LOCAL_HEADS):
        for j in range(GROUP):
            for to, at in head_rows(j):
                qs[to, ROWS * h : ROWS * (h + 1)] = q_ref[h, at]


def attend(base_ref, index_ref, q_ref, *refs):
    pieces, (p_ref, a_ref, qs, keys, values) = refs[:GROUP], refs[GROUP:]
    hold_spans(index_ref, pieces, keys, values)
    hold_queries(q_ref, qs)
    width = LOCAL_HEADS * ROWS
    key_at = lax.broadcasted_iota(jnp.int32, (ROWS, width), 0)
    query_at = lax.broadcasted_iota(jnp.int32, (ROWS, width), 1) % ROWS
    top = jnp.full((1, width), -1e30, F32)
    for i in range(TILES):
        lanes, exists = window(base_ref, i)
        scores = dot(keys[:, lanes], qs[...], 0, 0) * (HEAD_DIM**-0.5)
        if i == 0:
            scores = jnp.where((key_at > query_at) & exists, scores, -1e30)
        elif i == TILES - 1:
            scores = jnp.where(key_at <= query_at, scores, -1e30)
        else:
            scores = jnp.where(exists, scores, -1e30)
        p_ref[i] = scores
        top = jnp.maximum(top, jnp.max(scores, axis=0, keepdims=True))
    total = jnp.zeros((1, width), F32)
    for i in range(TILES):
        weights = jnp.exp(p_ref[i] - top)
        p_ref[i] = weights
        total = total + jnp.sum(weights, axis=0, keepdims=True)
    scale = 1.0 / total
    result = jnp.zeros((HEAD_DIM, width), F32)
    for i in range(TILES):
        lanes, _ = window(base_ref, i)
        probs = p_ref[i] * scale
        p_ref[i] = probs
        result = result + dot(values[:, lanes], probs.astype(BF), 1, 0)
    for h in range(LOCAL_HEADS):
        a_ref[h] = result[:, ROWS * h : ROWS * (h + 1)].astype(BF)


def attend_back(base_ref, index_ref, q_ref, p_ref, da_ref, *refs):
    pieces = refs[:GROUP]
    dq_ref, mine_ref, theirs_ref, qs, das, dps, keys, values, d_keys, d_values = refs[-10:]
    hold_spans(index_ref, pieces, keys, values)
    hold_queries(q_ref, qs)
    width = LOCAL_HEADS * ROWS
    for h in range(LOCAL_HEADS):
        das[:, ROWS * h : ROWS * (h + 1)] = da_ref[h]
    d_keys[...] = jnp.zeros(d_keys.shape, BF)
    d_values[...] = jnp.zeros(d_values.shape, BF)
    delta = jnp.zeros((1, width), F32)
    for i in range(TILES):
        lanes, _ = window(base_ref, i)
        probs = p_ref[i]
        d_probs = dot(values[:, lanes], das[...], 0, 0)
        dps[i] = d_probs
        delta = delta + jnp.sum(probs * d_probs, axis=0, keepdims=True)
        d_values[:, lanes] = dot(das[...], probs.astype(BF), 1, 1).astype(BF)
    dq = jnp.zeros((HEAD_DIM, width), F32)
    for i in range(TILES):
        lanes, _ = window(base_ref, i)
        d_scores = (p_ref[i] * (dps[i] - delta)).astype(BF)
        dq = dq + dot(keys[:, lanes], d_scores, 1, 0)
        d_keys[:, lanes] = (dot(qs[...], d_scores, 1, 1) * (HEAD_DIM**-0.5)).astype(BF)
    for h in range(LOCAL_HEADS):
        for j in range(GROUP):
            for at, to in head_rows(j):
                dq_ref[h, to] = dq[at, ROWS * h : ROWS * (h + 1)] * (HEAD_DIM**-0.5)
    core = base_ref[1] % 2
    for j in range(GROUP):
        rows = slice(2 * PART * j, 2 * PART * (j + 1))
        for ref, match in ((mine_ref, j % 2), (theirs_ref, 1 - j % 2)):

            @pl.when(core == match)
            def _(ref=ref, rows=rows, j=j):
                for back in range(3):
                    lanes = slice(1024 * (2 - back), 1024 * (3 - back))
                    ref[j // 2, back, : 2 * PART] = d_keys[rows, lanes]
                    ref[j // 2, back, 2 * PART :] = d_values[rows, lanes]


def project(x_ref, w_ref, n_ref, raw_ref, gains_ref):
    @pl.when(pl.program_id(0) == 0)
    def _():
        turned = w_ref[:, 128:].astype(F32).T
        at = Q_PART + KV_PART - 128
        gains_ref[...] = turned[at : at + 8]

    x = x_ref[...].reshape(2 * ROWS, D).astype(F32)
    normed = (x * rms_rate(x) * gains_ref[0:1]).astype(BF)
    n_ref[...] = normed.reshape(2, ROWS, D)
    raw_ref[...] = dot(normed, w_ref[...], 1, 0).T


def project_back(index_ref, sent_ref, w_ref, x_ref, mine_ref, theirs_ref, gain_ref, held):
    @pl.when(pl.program_id(0) == 0)
    def _():
        gain_ref[...] = jnp.zeros(gain_ref.shape, F32)

    sent = sent_ref[...].astype(F32).T.astype(BF)
    part = dot(sent, w_ref[:, : Q_PART + KV_PART], 1, 1)
    x = x_ref[...].reshape(2 * ROWS, D).astype(F32)
    gain_ref[0:1] += jnp.sum(part * x * rms_rate(x), axis=0, keepdims=True)
    held[...] = part.astype(BF).reshape(2, ROWS, D)
    mine_ref[0] = held[index_ref[C_AT]]
    theirs_ref[0] = held[index_ref[C_AT + 1]]


def chunk_grad(part):
    def body(index_ref, rows_ref, cols_ref, extra_ref, *refs):
        *out_refs, total, held = refs[-6:]
        step = pl.program_id(0)

        @pl.when(step == 0)
        def _():
            total[...] = jnp.zeros(total.shape, F32)
            total[part : part + 8] = extra_ref[...]

        total[:part] += dot(cols_ref[...], rows_ref[...].reshape(2 * ROWS, D), 1, 0)

        @pl.when(step == 3)
        def _():
            block, whole = GROUP * OWNED, total[...].T
            for k in range(8):
                held[k % 4, k // 4] = whole[k * block : (k + 1) * block].astype(BF)
            for k, out in enumerate(out_refs):
                out[...] = held[index_ref[Y_AT + (0, 2, 1, 3)[k]]]

    return body


def grad_by_chunk(rows, cols, extra, index, after=()):
    part = cols.shape[0]
    shape = (2, GROUP * OWNED, 256)
    return pl.pallas_call(
        chunk_grad(part),
        grid=(4,),
        out_shape=(jax.ShapeDtypeStruct(shape, BF),) * 4,
        in_specs=[
            SMEM,
            pl.BlockSpec((2, ROWS, D), lambda k: (k, 0, 0)),
            pl.BlockSpec((part, 2 * ROWS), lambda k: (0, k)),
            pl.BlockSpec((8, D), lambda k: (0, 0)),
        ]
        + [ANY] * len(after),
        out_specs=(pl.BlockSpec(shape, lambda k: (0, 0, 0)),) * 4,
        scratch_shapes=[
            pltpu.VMEM((256, D), F32),
            pltpu.VMEM((4, 2, GROUP * OWNED, 256), BF),
        ],
        cost_estimate=SMALL,
        compiler_params=params(32),
    )(index, rows, cols, extra, *after)


def row_scatter(parts, b):
    total = parts[0].astype(F32)
    for step, part in zip(STEPS[1:], parts[1:]):
        total = total + shift(part, "y", step).astype(F32)
    return pair_total(low_bits(total), 0, b, "b").astype(BF)


def rms_rate(values):
    return lax.rsqrt(jnp.mean(values * values, axis=-1, keepdims=True) + 1e-06)


def rotate(values, cosine, sine):
    first, second = values[..., 0, :, :], values[..., 1, :, :]
    return jnp.stack([first * cosine - second * sine, second * cosine + first * sine], axis=-3)


def local(
    tokens,
    cotangent,
    query_weight,
    query_moment,
    query_second,
    keyvalue_weight,
    keyvalue_moment,
    keyvalue_second,
    output_weight,
    output_moment,
    output_second,
    feedforward_weight,
    feedforward_moment,
    feedforward_second,
    norm_gains,
    gains_moment,
    gains_second,
):
    x, y, c, b = (lax.axis_index(name) for name in "xycb")
    j = 2 * x + c
    wide_rate = 1.5 * D**-0.5
    output_rate = 1.5 * (HEADS * HEAD_DIM // 32) ** -0.5
    index = jnp.stack(
        [(y + 4 - step) % 4 for step in STEPS] + [(x + 4 - step) % 4 for step in STEPS]
        + [b, 1 - b, c, 1 - c]
    ).astype(jnp.int32)
    base = jnp.stack([y, j]).astype(jnp.int32)

    inflow = tokens.astype(F32)
    parcel = jax.ShapeDtypeStruct((4, OWNED, 256), BF)
    parcels = pl.pallas_call(
        pack_small,
        out_shape=(parcel, parcel),
        in_specs=[SMEM] + [VMEM] * 3,
        out_specs=(VMEM, VMEM),
        scratch_shapes=[pltpu.VMEM((GROUP, OWNED, 256), BF)],
        cost_estimate=SMALL,
        compiler_params=params(16),
    )(index, query_weight, keyvalue_weight, norm_gains.T)
    small = group_exchange(*parcels, index).reshape(GROUP * OWNED, 256)
    group_tokens = lax.all_gather(tie(tokens, small), ("x", "c"), axis=0)
    partner = swap(small, "b")
    w_small = pair_gather(small, partner, "b", "y", index).reshape(D, 256)
    rows = tie(output_weight.astype(BF), w_small)
    rows = pair_gather(rows, swap(rows, "b"), "b", "y", index).reshape(8, OWNED, -1)
    parcel = jax.ShapeDtypeStruct((4, OWNED, 3 * F_PAD), BF)
    parcel_block = pl.BlockSpec((4, OWNED, F_PAD), lambda k: (0, 0, k))
    parcels = pl.pallas_call(
        pack_feed,
        grid=(3,),
        out_shape=(parcel, parcel),
        in_specs=[SMEM, pl.BlockSpec((1, OWNED, 8 * F_PART), lambda k: (k, 0, 0)), ANY],
        out_specs=(parcel_block, parcel_block),
        scratch_shapes=[pltpu.VMEM((GROUP, OWNED, F_PAD), BF)],
        cost_estimate=SMALL,
        compiler_params=params(24),
    )(index, feedforward_weight, partner)
    feed = exchange_sends(*parcels, (group_tokens, rows))
    feed = exchange_place(feed, index).reshape(GROUP * OWNED, 3 * F_PAD)
    feed_partner = swap(feed, "b")
    w_small = tie(w_small, feed)
    rows = tie(rows, group_tokens)
    rows_left, rows_right = shift(rows, "x", 1), shift(rows, "x", 3)

    token_block = pl.BlockSpec((2, ROWS, D), lambda k: (k, 0, 0))
    small_block = pl.BlockSpec((D, 256), lambda k: (0, 0))
    gains_block = pl.BlockSpec((8, D), lambda k: (0, 0))
    normed_a, raw, gains = pl.pallas_call(
        project,
        grid=(4,),
        out_shape=(
            jax.ShapeDtypeStruct((GROUP, ROWS, D), BF),
            jax.ShapeDtypeStruct((256, 1024), F32),
            jax.ShapeDtypeStruct((8, D), F32),
        ),
        in_specs=[token_block, small_block],
        out_specs=(token_block, pl.BlockSpec((256, 2 * ROWS), lambda k: (0, k)), gains_block),
        cost_estimate=SMALL,
        compiler_params=params(32),
    )(group_tokens, w_small)
    steps = jnp.arange(HEAD_DIM // 2, dtype=F32)
    freqs = jnp.exp(steps * (-2.0 * math.log(10000.0) / HEAD_DIM))
    first = y * 1024

    def turn(frequencies, first, count):
        places = (first + jnp.arange(count, dtype=jnp.int32)).astype(F32)
        angle = frequencies[:, None] * places[None, :]
        return jnp.cos(angle), jnp.sin(angle)

    group_turn = turn(lax.dynamic_slice_in_dim(freqs, PART * j, PART), first, 1024)
    own_turn = turn(freqs, first + ROWS * j, ROWS)
    keys = rotate(raw[Q_PART : Q_PART + 2 * PART].reshape(2, PART, 1024), *group_turn)
    values = raw[Q_PART + 2 * PART : Q_PART + KV_PART].reshape(2, PART, 1024)
    pair = jnp.concatenate([keys, values]).astype(BF).reshape(KV_PART, 1024)
    pair_back = [push(pair, "y", 1), push(pair, "y", 2)]
    q_raw = raw[:Q_PART].astype(BF).reshape(Q_PART, GROUP, ROWS).transpose(1, 0, 2)
    q_raw = exchange(q_raw)
    feed_partner = tie(feed_partner, *pair_back)
    pair_back[0] = tie(pair_back[0], q_raw, rows_left, rows_right)
    rows_left, rows_right = tie(rows_left, q_raw), tie(rows_right, q_raw)
    rows_top, rows_bottom = shift(rows_left[:4], "x", 1), shift(rows_right[4:], "x", 3)
    q_raw = q_raw.astype(F32).reshape(LOCAL_HEADS, 2, HEAD_DIM // 2, ROWS)
    queries = rotate(q_raw, *own_turn).astype(BF).reshape(LOCAL_HEADS, HEAD_DIM, ROWS)
    spans = direct(jnp.stack([pair] + pair_back), "x")
    feed_pair = both_in_order(feed, feed_partner, b)
    w_feed = lax.all_gather(feed_pair, "y", axis=1, tiled=True).reshape(D, 3 * F_PAD)
    back_pieces = direct(tie(cotangent, *spans[1:]), "x")
    spans = spans + [swap(piece, "c") for piece in spans]
    rows_top = tie(rows_top, *spans[5:])
    w_output = place_rows([rows, rows_left, rows_right, rows_top, rows_bottom], index)

    width = LOCAL_HEADS * ROWS
    held_spans = [pltpu.VMEM((HEAD_DIM, 3072), BF)] * 2
    probs, attended = pl.pallas_call(
        attend,
        out_shape=(
            jax.ShapeDtypeStruct((TILES, ROWS, width), F32),
            jax.ShapeDtypeStruct((LOCAL_HEADS, HEAD_DIM, ROWS), BF),
        ),
        in_specs=[SMEM, SMEM] + [VMEM] * 9,
        out_specs=(VMEM, VMEM),
        scratch_shapes=[pltpu.VMEM((HEAD_DIM, width), BF)] + held_spans,
        cost_estimate=SMALL,
        compiler_params=params(40),
    )(base, index, queries, *spans)
    attended = attended.reshape(LOCAL_HEADS * HEAD_DIM, ROWS)
    branch = low_bits(dot(attended, w_output, 0, 1))
    back_pieces[1:] = [tie(piece, branch) for piece in back_pieces[1:]]
    other_branch = tie(swap(branch, "t"), *back_pieces[1:])
    residual = inflow + (branch.astype(F32) + other_branch.astype(F32))

    rate_b = rms_rate(residual)
    normed_b = tie((residual * rate_b * gains[1]).astype(BF), w_feed)
    group_b = lax.all_gather(normed_b, ("x", "c"), axis=0).reshape(1024, D)
    group_back = group_place(back_pieces, index).reshape(1024, D)
    d_hidden = dot(group_back, w_feed[:, 2 * F_PAD :], 1, 0)
    gate_up = dot(group_b, w_feed[:, : 2 * F_PAD], 1, 0)
    gate, up = gate_up[:, :F_PAD], gate_up[:, F_PAD:]
    root = math.sqrt(2.0 / math.pi)
    bend = jnp.tanh(root * (gate + 0.044715 * gate * gate * gate))
    gelu = 0.5 * gate * (1.0 + bend)
    slope = 0.5 * (1.0 + bend) + 0.5 * gate * (1.0 - bend * bend) * root * (
        1.0 + 3.0 * 0.044715 * gate * gate
    )
    hidden = (gelu * up).astype(BF)
    d_gate_up = jnp.concatenate(
        [(d_hidden * up * slope).astype(BF), (d_hidden * gelu).astype(BF)], axis=1
    )
    normb_part = low_bits(dot(d_gate_up, w_feed[:, : 2 * F_PAD], 1, 1))
    normb_low = lax.psum_scatter(
        normb_part.reshape(GROUP, ROWS, D), ("x", "c"), scatter_dimension=0
    )
    down_grad = dot(tie(group_back, normb_part), hidden, 0, 0).astype(BF)
    gate_grad = dot(tie(group_b, normb_part), d_gate_up, 0, 0).astype(BF)
    feed_part = low_bits(dot(hidden, w_feed[:, 2 * F_PAD :], 1, 1)).reshape(GROUP, ROWS, D)
    normb_low = tie(normb_low, down_grad, gate_grad, feed_part)
    grad_normb = tensor_sum(normb_low)
    feed_grad = jnp.concatenate([gate_grad, down_grad], axis=1).reshape(2, -1, 3 * F_PAD)
    feed_grad = lax.psum_scatter(feed_grad, "y", scatter_dimension=1, tiled=True)
    scaled = grad_normb * gains[1]
    grad_resid = (
        cotangent.astype(F32)
        + rate_b * scaled
        - residual * rate_b**3 * jnp.mean(scaled * residual, axis=-1, keepdims=True)
    )
    gain_b = jnp.sum(grad_normb * residual * rate_b, axis=0)
    resid_low = grad_resid.astype(BF)
    grad_att = dot(w_output, resid_low, 0, 1).astype(BF).reshape(LOCAL_HEADS, HEAD_DIM, ROWS)

    span_parts = jax.ShapeDtypeStruct((4, 3, KV_PART, 1024), BF)
    grad_q, span_mine, span_theirs = pl.pallas_call(
        attend_back,
        out_shape=(
            jax.ShapeDtypeStruct((LOCAL_HEADS, HEAD_DIM, ROWS), F32),
            span_parts,
            span_parts,
        ),
        in_specs=[SMEM, SMEM] + [VMEM] * 11,
        out_specs=(VMEM, VMEM, VMEM),
        scratch_shapes=[
            pltpu.VMEM((HEAD_DIM, width), BF),
            pltpu.VMEM((HEAD_DIM, width), BF),
            pltpu.VMEM((TILES, ROWS, width), F32),
        ]
        + held_spans * 2,
        cost_estimate=SMALL,
        compiler_params=params(44),
    )(base, index, queries, probs, grad_att, *spans)
    query_grad = (
        rotate(grad_q.reshape(LOCAL_HEADS, 2, HEAD_DIM // 2, ROWS), own_turn[0], -own_turn[1])
        .astype(BF)
        .reshape(GROUP, Q_PART, ROWS)
    )
    moved = jnp.concatenate([query_grad, attended.reshape(GROUP, Q_PART, ROWS)], axis=1)
    moved = exchange(moved).transpose(1, 0, 2).reshape(2 * Q_PART, 1024)
    query_grad, group_attended = moved[:Q_PART], moved[Q_PART:]
    back_terms = scatter_terms(span_mine, span_theirs, "c", "x", index)
    back_terms[1] = tie(back_terms[1], moved)
    back = total_of(back_terms)
    back = (
        back[0]
        + push(back[1].astype(BF), "y", -1).astype(F32)
        + push(back[2].astype(BF), "y", -2).astype(F32)
    )
    grad_k = rotate(back[: 2 * PART].reshape(2, PART, 1024), group_turn[0], -group_turn[1])
    grad_v = back[2 * PART :].reshape(2, PART, 1024)
    pair_grad = jnp.concatenate([grad_k, grad_v]).astype(BF).reshape(KV_PART, 1024)

    sent = jnp.concatenate([query_grad, pair_grad])
    feed_grad = tie(feed_grad, sent)
    group_resid = lax.all_gather(tie(resid_low, feed_grad), ("x", "c"), axis=0)
    feed_grad = pair_total(feed_grad, 0, b, "b").astype(BF)
    side = jax.ShapeDtypeStruct((4, ROWS, D), BF)
    side_block = pl.BlockSpec((1, ROWS, D), lambda k: (k, 0, 0))
    norma_mine, norma_theirs, gain_a = pl.pallas_call(
        project_back,
        grid=(4,),
        out_shape=(side, side, jax.ShapeDtypeStruct((8, D), F32)),
        in_specs=[
            SMEM,
            pl.BlockSpec((Q_PART + KV_PART, 2 * ROWS), lambda k: (0, k)),
            small_block,
            token_block,
        ],
        out_specs=(side_block, side_block, gains_block),
        scratch_shapes=[pltpu.VMEM((2, ROWS, D), BF)],
        cost_estimate=SMALL,
        compiler_params=params(32),
    )(index, sent, w_small, group_tokens)
    rate_a = rms_rate(inflow)
    norma_terms = scatter_terms(norma_mine, norma_theirs, "c", "x", index)
    extra = jnp.concatenate([gain_a[:1], 0.5 * gain_b[None], jnp.zeros((6, D), F32)])
    small_parts = grad_by_chunk(normed_a, sent, extra, index, (norma_terms[0],))
    small_grad = row_scatter(small_parts, b)
    norma_terms[1:] = [tie(term, small_grad, feed_grad) for term in norma_terms[1:]]
    late = jnp.concatenate([feed_grad, small_grad], axis=1)
    late = exchange(late.reshape(GROUP, OWNED, 3 * F_PAD + 256))
    feed_grad, small_grad = late, late[:, :, 3 * F_PAD :]
    norma_low = low_bits(total_of(norma_terms))
    output_parts = grad_by_chunk(
        group_resid, group_attended, jnp.zeros((8, D), F32), index, (norma_low,)
    )
    out_low = lax.psum_scatter(
        tie(feed_part, norma_low, output_parts[0]), ("x", "c"), scatter_dimension=0
    )
    other_out = swap(out_low, "t")
    out_tokens = (residual + (out_low.astype(F32) + other_out.astype(F32))).astype(BF)
    grad_norma = tensor_sum(norma_low)
    scaled = grad_norma * gains[0]
    input_grad = (
        grad_resid
        + rate_a * scaled
        - inflow * rate_a**3 * jnp.mean(scaled * inflow, axis=-1, keepdims=True)
    )

    output_grad = exchange(row_scatter(output_parts, b).reshape(GROUP, OWNED, 256))

    def update(grads, weight, moment, second, part, start, rate, pair=False):
        return pl.pallas_call(
            adam_columns(part, start, rate, pair),
            out_shape=(jax.ShapeDtypeStruct(weight.shape, F32),) * 3,
            in_specs=[VMEM] * (3 + len(grads)),
            out_specs=(VMEM,) * 3,
            cost_estimate=SMALL,
            compiler_params=params(32),
        )(*grads, weight, moment, second)

    other_grad = swap(small_grad, "t")
    query_new = update([small_grad], query_weight, query_moment, query_second, Q_PART, 0, wide_rate)
    pair_new = update(
        [small_grad, other_grad],
        keyvalue_weight,
        keyvalue_moment,
        keyvalue_second,
        KV_PART,
        Q_PART,
        wide_rate,
        True,
    )
    output_new = update(
        [output_grad], output_weight, output_moment, output_second, Q_PART, 0, output_rate
    )
    matrix = pl.BlockSpec((1, OWNED, 8 * F_PART), lambda k: (k, 0, 0))
    feed_new = pl.pallas_call(
        adam_columns(F_PART, 0, wide_rate),
        grid=(3,),
        out_shape=(jax.ShapeDtypeStruct(feedforward_weight.shape, F32),) * 3,
        in_specs=[pl.BlockSpec((GROUP, OWNED, F_PAD), lambda k: (0, 0, k))] + [matrix] * 3,
        out_specs=(matrix,) * 3,
        cost_estimate=SMALL,
        compiler_params=params(32),
    )(feed_grad, feedforward_weight, feedforward_moment, feedforward_second)
    gain_grad = small_grad.astype(F32) + other_grad.astype(F32)
    gain_grad = jnp.sum(gain_grad[:, :, Q_PART + KV_PART : Q_PART + KV_PART + 2], axis=0).T
    gains_new = adam(norm_gains, gain_grad, gains_moment, gains_second, 0.3, 0.0)
    return (
        out_tokens,
        input_grad,
        *query_new,
        *pair_new,
        *output_new,
        *feed_new,
        *gains_new,
    )


def solution(mesh):
    grid = Mesh(mesh.devices.reshape(2, 4, 4, 2, 2), ("b", "y", "x", "c", "t"))
    rows = ("b", "y", "x", "c")
    token = P(rows, None)
    split = P(rows, "t")
    whole = P(rows, None)
    feed = P(None, rows, "t")
    gain = P(None, rows)
    weights = (split,) * 3 + (whole,) * 3 + (split,) * 3 + (feed,) * 3 + (gain,) * 3
    return jax.shard_map(
        local,
        mesh=grid,
        in_specs=(token, token) + weights,
        out_specs=(token, token) + weights,
        check_vma=False,
    )
```

```python
import math

import jax
import jax.numpy as jnp
from jax import lax
from jax.experimental import pallas as pl
from jax.experimental.pallas import tpu as pltpu
from jax.sharding import Mesh
from jax.sharding import PartitionSpec as P

D = 2560
HEADS = 10
HEAD_DIM = 256
STEP = 10
ROWS = 128
GROUP = 8
OWNED = 40
Q_PART = 160
KV_PART = 64
F_PART = 480
F_PAD = 512
LOCAL_HEADS = 5
TILES = 17
BF = jnp.bfloat16
F32 = jnp.float32
ANY = pl.BlockSpec(memory_space=pl.ANY)
SMEM = pl.BlockSpec(memory_space=pltpu.SMEM)
VMEM = pl.BlockSpec(memory_space=pltpu.VMEM)


SMALL = pl.CostEstimate(flops=1, transcendentals=0, bytes_accessed=1)


def params(mib):
    return pltpu.CompilerParams(vmem_limit_bytes=mib * 1024 * 1024)


def dot(left, right, left_dim, right_dim):
    return lax.dot_general(
        left, right, (((left_dim,), (right_dim,)), ((), ())), preferred_element_type=F32
    )


def shift(value, axis, step):
    return lax.ppermute(value, axis, [(i, (i + step) % 4) for i in range(4)])


def push(value, axis, step):
    return lax.ppermute(value, axis, [(i, i + step) for i in range(4) if 0 <= i + step < 4])


def swap(value, axis):
    return lax.ppermute(value, axis, [(0, 1), (1, 0)])


STEPS = (0, 1, 3, 2)
Y_AT, X_AT, B_AT, C_AT = 0, 4, 8, 10


def tie(value, *others):
    def body(*refs):
        del refs

    return pl.pallas_call(
        body,
        out_shape=jax.ShapeDtypeStruct(value.shape, value.dtype),
        in_specs=[ANY] * (1 + len(others)),
        out_specs=ANY,
        input_output_aliases={0: 0},
        cost_estimate=SMALL,
    )(value, *others)


def place(pieces, index, shape, target):
    count = len(pieces)

    def body(index_ref, *refs):
        out, sems = refs[count], refs[count + 1]
        copies = [
            pltpu.make_async_copy(refs[k], target(out, index_ref, k), sems.at[k])
            for k in range(count)
        ]
        for copy in copies:
            copy.start()
        for copy in copies:
            copy.wait()

    return pl.pallas_call(
        body,
        out_shape=jax.ShapeDtypeStruct(shape, pieces[0].dtype),
        in_specs=[SMEM] + [VMEM] * count,
        out_specs=ANY,
        scratch_shapes=[pltpu.SemaphoreType.DMA((count,))],
        cost_estimate=SMALL,
        compiler_params=params(24),
    )(index, *pieces)


def direct(value, axis):
    return [value] + [shift(value, axis, step) for step in STEPS[1:]]


def group_place(mine, index):
    pieces = mine + [swap(piece, "c") for piece in mine]

    def target(out, index_ref, k):
        return out.at[2 * index_ref[X_AT + k % 4] + index_ref[C_AT + k // 4]]

    return place(pieces, index, (GROUP,) + mine[0].shape, target)


def group_gather(value, index):
    return group_place(direct(value, "x"), index)


def two_step_gather(value, index):
    half = value.shape[0] // 2
    left, right = shift(value, "x", 1), shift(value, "x", 3)
    top, bottom = shift(left[:half], "x", 1), shift(right[half:], "x", 3)
    mine = [value, left, right, top, bottom]
    pieces = mine + [swap(piece, "c") for piece in mine]
    pieces = [
        piece if k % 5 > 2 else piece.reshape((2, half) + value.shape[1:])
        for k, piece in enumerate(pieces)
    ]

    def target(out, index_ref, k):
        spot = 2 * index_ref[X_AT + min(k % 5, 3)] + index_ref[C_AT + k // 5]
        return out.at[spot] if k % 5 < 3 else out.at[spot, k % 5 - 3]

    out = place(pieces, index, (GROUP, 2, half) + value.shape[1:], target)
    return out.reshape((GROUP,) + value.shape), (left, right)


def place_rows(mine, index):
    pieces = mine + [swap(piece, "c") for piece in mine]

    def target(out, index_ref, k):
        spot = 2 * index_ref[X_AT + min(k % 5, 3)] + index_ref[C_AT + k // 5]
        if k % 5 < 3:
            return out.at[:, spot]
        return out.at[pl.ds((k % 5 - 3) * 4, 4), spot]

    width = mine[0].shape[2]
    return place(pieces, index, (8, GROUP, OWNED, width), target).reshape(D, width)


def pair_gather(mine, theirs, pair_axis, ring_axis, index, after=()):
    pieces = direct(jnp.stack([mine, theirs]), ring_axis)
    ring_at, pair_at = (X_AT, C_AT) if ring_axis == "x" else (Y_AT, B_AT)

    def body(index_ref, *refs):
        out, sems = refs[-2:]
        copies = []
        for k in range(4):
            for h in range(2):
                spot, side = index_ref[ring_at + k], index_ref[pair_at + h]
                to = out.at[spot, side] if ring_axis == "x" else out.at[side, spot]
                copies.append(pltpu.make_async_copy(refs[k].at[h], to, sems.at[2 * k + h]))
        for copy in copies:
            copy.start()
        for copy in copies:
            copy.wait()

    shape = ((4, 2) if ring_axis == "x" else (2, 4)) + mine.shape
    return pl.pallas_call(
        body,
        out_shape=jax.ShapeDtypeStruct(shape, mine.dtype),
        in_specs=[SMEM] + [VMEM] * 4 + [ANY] * len(after),
        out_specs=ANY,
        scratch_shapes=[pltpu.SemaphoreType.DMA((8,))],
        cost_estimate=SMALL,
        compiler_params=params(16),
    )(index, *pieces, *after)


def exchange_sends(mine, theirs, after=()):
    pair = jnp.stack([mine, swap(theirs, "c")], axis=1)
    if after:
        pair = tie(pair, *after)
    return [pair[0]] + [shift(pair[k], "x", STEPS[k]) for k in range(1, 4)]


def exchange_place(pieces, index):
    def body(index_ref, *refs):
        out, sems = refs[-2:]
        copies = []
        for k in range(4):
            for h in range(2):
                to = out.at[index_ref[X_AT + k], index_ref[C_AT + h]]
                copies.append(pltpu.make_async_copy(refs[k].at[h], to, sems.at[2 * k + h]))
        for copy in copies:
            copy.start()
        for copy in copies:
            copy.wait()

    return pl.pallas_call(
        body,
        out_shape=jax.ShapeDtypeStruct((4, 2) + pieces[0].shape[1:], pieces[0].dtype),
        in_specs=[SMEM] + [VMEM] * 4,
        out_specs=ANY,
        scratch_shapes=[pltpu.SemaphoreType.DMA((8,))],
        cost_estimate=SMALL,
        compiler_params=params(16),
    )(index, *pieces)


def group_exchange(mine, theirs, index):
    return exchange_place(exchange_sends(mine, theirs), index)


def fold(mine, received, index, at, after=()):
    shape = mine.shape[1:]

    def body(index_ref, mine_ref, received_ref, *refs):
        for k, out in enumerate(refs[len(after) :]):
            spot = index_ref[at + (0, 2, 1, 3)[k]]
            total = mine_ref[spot].astype(F32) + received_ref[spot].astype(F32)
            out[...] = total.astype(out.dtype)

    return pl.pallas_call(
        body,
        out_shape=(jax.ShapeDtypeStruct(shape, F32),) + (jax.ShapeDtypeStruct(shape, BF),) * 3,
        in_specs=[SMEM, VMEM, VMEM] + [ANY] * len(after),
        out_specs=(VMEM,) * 4,
        cost_estimate=SMALL,
        compiler_params=params(40),
    )(index, mine, received, *after)


def scatter_terms(mine, theirs, pair_axis, ring_axis, index, after=()):
    at = X_AT if ring_axis == "x" else Y_AT
    own, *others = fold(mine, swap(theirs, pair_axis), index, at, after)
    return [own] + [shift(other, ring_axis, step) for step, other in zip(STEPS[1:], others)]


def total_of(terms):
    return sum(term.astype(F32) for term in terms)


def scatter(*args, **kwargs):
    return total_of(scatter_terms(*args, **kwargs))


def pair_total(parts, axis, place_at, pair_axis):
    mine, theirs = sides(parts, axis, place_at)
    return mine.astype(F32) + swap(theirs, pair_axis).astype(F32)


def sides(parts, axis, place_at):
    return (
        lax.dynamic_index_in_dim(parts, place_at, axis, keepdims=False),
        lax.dynamic_index_in_dim(parts, 1 - place_at, axis, keepdims=False),
    )


def both_in_order(mine, theirs, place_at):
    first = place_at == 0
    return jnp.stack([jnp.where(first, mine, theirs), jnp.where(first, theirs, mine)])


def low_bits(value):
    return lax.optimization_barrier(value.astype(BF))


def tensor_sum(low):
    return low.astype(F32) + swap(low, "t").astype(F32)


def exchange(value):
    return lax.all_to_all(value, ("x", "c"), split_axis=0, concat_axis=0, tiled=True)


def hand_out(index_ref, held, mine_ref, theirs_ref):
    for k in range(4):
        spot = 2 * index_ref[X_AT + (0, 2, 1, 3)[k]]
        mine_ref[k] = held[spot + index_ref[C_AT]]
        theirs_ref[k] = held[spot + index_ref[C_AT + 1]]


def pack_small(index_ref, q_ref, kv_ref, gain_ref, mine_ref, theirs_ref, held):
    rest = jnp.zeros((OWNED, 256 - Q_PART - KV_PART - 2), F32)
    half, part = HEAD_DIM // 2, KV_PART // 4
    for j in range(GROUP):
        held[j] = jnp.concatenate(
            [
                q_ref[:, Q_PART * j : Q_PART * (j + 1)],
                kv_ref[:, part * j : part * (j + 1)],
                kv_ref[:, half + part * j : half + part * (j + 1)],
                kv_ref[:, 2 * half + 2 * part * j : 2 * half + 2 * part * (j + 1)],
                gain_ref[...],
                rest,
            ],
            axis=1,
        ).astype(BF)
    hand_out(index_ref, held, mine_ref, theirs_ref)


def pack_feed(index_ref, w_ref, after_ref, mine_ref, theirs_ref, held):
    del after_ref
    rest = jnp.zeros((OWNED, F_PAD - F_PART), F32)
    for j in range(GROUP):
        held[j] = jnp.concatenate(
            [w_ref[0, :, F_PART * j : F_PART * (j + 1)], rest], axis=1
        ).astype(BF)
    hand_out(index_ref, held, mine_ref, theirs_ref)


def adam(weight, grad, moment, second, rate, decay):
    moment_new = 0.9 * moment + 0.1 * grad
    second_new = 0.95 * second + 0.05 * grad * grad
    ratio = moment_new / (1.0 - 0.9**STEP) / (jnp.sqrt(second_new / (1.0 - 0.95**STEP)) + 1e-08)
    return (moment_new, second_new, weight - rate * (ratio + decay * weight))


def adam_columns(part, start, rate, pair=False):
    if pair:
        cuts = [(start, PART), (start + PART, PART), (start + 2 * PART, 2 * PART)]
    else:
        cuts = [(start, part)]

    def body(*refs):
        *g_refs, w_ref, m_ref, v_ref, mo_ref, vo_ref, wo_ref = refs
        grad = sum(
            jnp.concatenate(
                [
                    g_ref[j, :, at : at + count].astype(F32)
                    for at, count in cuts
                    for j in range(GROUP)
                ],
                axis=1,
            )
            for g_ref in g_refs
        )
        index = (0,) if len(w_ref.shape) == 3 else (slice(None),)
        m, v, w = adam(w_ref[index], grad, m_ref[index], v_ref[index], rate, 0.1)
        mo_ref[index] = m
        vo_ref[index] = v
        wo_ref[index] = w

    return body


def window(base_ref, i):
    start = pl.multiple_of(ROWS * (base_ref[1] + i), ROWS)
    return pl.ds(start, ROWS), base_ref[0] * 8 + base_ref[1] + i >= 16


PART = HEAD_DIM // 16


def head_rows(j):
    return (
        (slice(2 * PART * j, 2 * PART * j + PART), slice(PART * j, PART * j + PART)),
        (
            slice(2 * PART * j + PART, 2 * PART * (j + 1)),
            slice(HEAD_DIM // 2 + PART * j, HEAD_DIM // 2 + PART * (j + 1)),
        ),
    )


def hold_spans(index_ref, pieces, keys, values):
    for k, piece in enumerate(pieces):
        spot = 2 * index_ref[X_AT + k % 4] + index_ref[C_AT + k // 4]
        rows = pl.ds(pl.multiple_of(2 * PART * spot, 2 * PART), 2 * PART)
        for back in range(3):
            lanes = slice(1024 * (2 - back), 1024 * (3 - back))
            keys[rows, lanes] = piece[back, : 2 * PART]
            values[rows, lanes] = piece[back, 2 * PART :]


def hold_queries(q_ref, qs):
    for h in range(LOCAL_HEADS):
        for j in range(GROUP):
            for to, at in head_rows(j):
                qs[to, ROWS * h : ROWS * (h + 1)] = q_ref[h, at]


def attend(base_ref, index_ref, q_ref, *refs):
    pieces, (p_ref, a_ref, qs, keys, values) = refs[:GROUP], refs[GROUP:]
    hold_spans(index_ref, pieces, keys, values)
    hold_queries(q_ref, qs)
    width = LOCAL_HEADS * ROWS
    key_at = lax.broadcasted_iota(jnp.int32, (ROWS, width), 0)
    query_at = lax.broadcasted_iota(jnp.int32, (ROWS, width), 1) % ROWS
    top = jnp.full((1, width), -1e30, F32)
    for i in range(TILES):
        lanes, exists = window(base_ref, i)
        scores = dot(keys[:, lanes], qs[...], 0, 0) * (HEAD_DIM**-0.5)
        if i == 0:
            scores = jnp.where((key_at > query_at) & exists, scores, -1e30)
        elif i == TILES - 1:
            scores = jnp.where(key_at <= query_at, scores, -1e30)
        else:
            scores = jnp.where(exists, scores, -1e30)
        p_ref[i] = scores
        top = jnp.maximum(top, jnp.max(scores, axis=0, keepdims=True))
    total = jnp.zeros((1, width), F32)
    for i in range(TILES):
        weights = jnp.exp(p_ref[i] - top)
        p_ref[i] = weights
        total = total + jnp.sum(weights, axis=0, keepdims=True)
    scale = 1.0 / total
    result = jnp.zeros((HEAD_DIM, width), F32)
    for i in range(TILES):
        lanes, _ = window(base_ref, i)
        probs = p_ref[i] * scale
        p_ref[i] = probs
        result = result + dot(values[:, lanes], probs.astype(BF), 1, 0)
    for h in range(LOCAL_HEADS):
        a_ref[h] = result[:, ROWS * h : ROWS * (h + 1)].astype(BF)


def attend_back(base_ref, index_ref, q_ref, p_ref, da_ref, *refs):
    pieces = refs[:GROUP]
    dq_ref, mine_ref, theirs_ref, qs, das, dps, keys, values, d_keys, d_values = refs[-10:]
    hold_spans(index_ref, pieces, keys, values)
    hold_queries(q_ref, qs)
    width = LOCAL_HEADS * ROWS
    for h in range(LOCAL_HEADS):
        das[:, ROWS * h : ROWS * (h + 1)] = da_ref[h]
    d_keys[...] = jnp.zeros(d_keys.shape, BF)
    d_values[...] = jnp.zeros(d_values.shape, BF)
    delta = jnp.zeros((1, width), F32)
    for i in range(TILES):
        lanes, _ = window(base_ref, i)
        probs = p_ref[i]
        d_probs = dot(values[:, lanes], das[...], 0, 0)
        dps[i] = d_probs
        delta = delta + jnp.sum(probs * d_probs, axis=0, keepdims=True)
        d_values[:, lanes] = dot(das[...], probs.astype(BF), 1, 1).astype(BF)
    dq = jnp.zeros((HEAD_DIM, width), F32)
    for i in range(TILES):
        lanes, _ = window(base_ref, i)
        d_scores = (p_ref[i] * (dps[i] - delta)).astype(BF)
        dq = dq + dot(keys[:, lanes], d_scores, 1, 0)
        d_keys[:, lanes] = (dot(qs[...], d_scores, 1, 1) * (HEAD_DIM**-0.5)).astype(BF)
    for h in range(LOCAL_HEADS):
        for j in range(GROUP):
            for at, to in head_rows(j):
                dq_ref[h, to] = dq[at, ROWS * h : ROWS * (h + 1)] * (HEAD_DIM**-0.5)
    core = base_ref[1] % 2
    for j in range(GROUP):
        rows = slice(2 * PART * j, 2 * PART * (j + 1))
        for ref, match in ((mine_ref, j % 2), (theirs_ref, 1 - j % 2)):

            @pl.when(core == match)
            def _(ref=ref, rows=rows, j=j):
                for back in range(3):
                    lanes = slice(1024 * (2 - back), 1024 * (3 - back))
                    ref[j // 2, back, : 2 * PART] = d_keys[rows, lanes]
                    ref[j // 2, back, 2 * PART :] = d_values[rows, lanes]


def project(x_ref, w_ref, n_ref, raw_ref, gains_ref):
    @pl.when(pl.program_id(0) == 0)
    def _():
        turned = w_ref[:, 128:].astype(F32).T
        at = Q_PART + KV_PART - 128
        gains_ref[...] = turned[at : at + 8]

    x = x_ref[...].reshape(2 * ROWS, D).astype(F32)
    normed = (x * rms_rate(x) * gains_ref[0:1]).astype(BF)
    n_ref[...] = normed.reshape(2, ROWS, D)
    raw_ref[...] = dot(normed, w_ref[...], 1, 0).T


def project_back(index_ref, sent_ref, w_ref, x_ref, mine_ref, theirs_ref, gain_ref, held):
    @pl.when(pl.program_id(0) == 0)
    def _():
        gain_ref[...] = jnp.zeros(gain_ref.shape, F32)

    sent = sent_ref[...].astype(F32).T.astype(BF)
    part = dot(sent, w_ref[:, : Q_PART + KV_PART], 1, 1)
    x = x_ref[...].reshape(2 * ROWS, D).astype(F32)
    gain_ref[0:1] += jnp.sum(part * x * rms_rate(x), axis=0, keepdims=True)
    held[...] = part.astype(BF).reshape(2, ROWS, D)
    mine_ref[0] = held[index_ref[C_AT]]
    theirs_ref[0] = held[index_ref[C_AT + 1]]


def chunk_grads(index_ref, rows_ref, cols_ref, extra_ref, rows2_ref, cols2_ref, after_ref, *refs):
    del after_ref
    *out_refs, total, held = refs
    step, part, part2 = pl.program_id(0), cols_ref.shape[0], cols2_ref.shape[0]

    @pl.when(step == 0)
    def _():
        total[...] = jnp.zeros(total.shape, F32)
        total[part : part + 8] = extra_ref[...]

    @pl.when(step < 4)
    def _():
        total[:part] += dot(cols_ref[...], rows_ref[...].reshape(2 * ROWS, D), 1, 0)

    @pl.when(step >= 4)
    def _():
        rows = rows2_ref[...].reshape(2 * ROWS, D)
        total[256 : 256 + part2] += dot(cols2_ref[...], rows, 1, 0)

    @pl.when(step == 7)
    def _():
        block, whole = GROUP * OWNED, total[...].T
        for k in range(8):
            held[k % 4, k // 4] = whole[k * block : (k + 1) * block].astype(BF)
        for k, out in enumerate(out_refs):
            out[...] = held[index_ref[Y_AT + (0, 2, 1, 3)[k]]]


def grads_by_chunk(rows, cols, extra, rows2, cols2, index, after):
    shape = (2, GROUP * OWNED, 512)

    def first(k):
        return jnp.minimum(k, 3)

    def second(k):
        return jnp.maximum(k - 4, 0)

    return pl.pallas_call(
        chunk_grads,
        grid=(8,),
        out_shape=(jax.ShapeDtypeStruct(shape, BF),) * 4,
        in_specs=[
            SMEM,
            pl.BlockSpec((2, ROWS, D), lambda k: (first(k), 0, 0)),
            pl.BlockSpec((cols.shape[0], 2 * ROWS), lambda k: (0, first(k))),
            pl.BlockSpec((8, D), lambda k: (0, 0)),
            pl.BlockSpec((2, ROWS, D), lambda k: (second(k), 0, 0)),
            pl.BlockSpec((cols2.shape[0], 2 * ROWS), lambda k: (0, second(k))),
            ANY,
        ],
        out_specs=(pl.BlockSpec(shape, lambda k: (0, 0, 0)),) * 4,
        scratch_shapes=[
            pltpu.VMEM((512, D), F32),
            pltpu.VMEM((4, 2, GROUP * OWNED, 512), BF),
        ],
        cost_estimate=SMALL,
        compiler_params=params(40),
    )(index, rows, cols, extra, rows2, cols2, after)


def row_scatter(parts, b):
    total = parts[0].astype(F32)
    for step, part in zip(STEPS[1:], parts[1:]):
        total = total + shift(part, "y", step).astype(F32)
    return pair_total(low_bits(total), 0, b, "b").astype(BF)


def rms_rate(values):
    return lax.rsqrt(jnp.mean(values * values, axis=-1, keepdims=True) + 1e-06)


def rotate(values, cosine, sine):
    first, second = values[..., 0, :, :], values[..., 1, :, :]
    return jnp.stack([first * cosine - second * sine, second * cosine + first * sine], axis=-3)


def local(
    tokens,
    cotangent,
    query_weight,
    query_moment,
    query_second,
    keyvalue_weight,
    keyvalue_moment,
    keyvalue_second,
    output_weight,
    output_moment,
    output_second,
    feedforward_weight,
    feedforward_moment,
    feedforward_second,
    norm_gains,
    gains_moment,
    gains_second,
):
    x, y, c, b = (lax.axis_index(name) for name in "xycb")
    j = 2 * x + c
    wide_rate = 1.5 * D**-0.5
    output_rate = 1.5 * (HEADS * HEAD_DIM // 32) ** -0.5
    index = jnp.stack(
        [(y + 4 - step) % 4 for step in STEPS] + [(x + 4 - step) % 4 for step in STEPS]
        + [b, 1 - b, c, 1 - c]
    ).astype(jnp.int32)
    base = jnp.stack([y, j]).astype(jnp.int32)

    inflow = tokens.astype(F32)
    parcel = jax.ShapeDtypeStruct((4, OWNED, 256), BF)
    parcels = pl.pallas_call(
        pack_small,
        out_shape=(parcel, parcel),
        in_specs=[SMEM] + [VMEM] * 3,
        out_specs=(VMEM, VMEM),
        scratch_shapes=[pltpu.VMEM((GROUP, OWNED, 256), BF)],
        cost_estimate=SMALL,
        compiler_params=params(16),
    )(index, query_weight, keyvalue_weight, norm_gains.T)
    small = group_exchange(*parcels, index).reshape(GROUP * OWNED, 256)
    group_tokens = lax.all_gather(tie(tokens, small), ("x", "c"), axis=0)
    partner = swap(small, "b")
    w_small = pair_gather(small, partner, "b", "y", index).reshape(D, 256)
    rows = tie(output_weight.astype(BF), w_small)
    rows = pair_gather(rows, swap(rows, "b"), "b", "y", index).reshape(8, OWNED, -1)
    parcel = jax.ShapeDtypeStruct((4, OWNED, 3 * F_PAD), BF)
    parcel_block = pl.BlockSpec((4, OWNED, F_PAD), lambda k: (0, 0, k))
    parcels = pl.pallas_call(
        pack_feed,
        grid=(3,),
        out_shape=(parcel, parcel),
        in_specs=[SMEM, pl.BlockSpec((1, OWNED, 8 * F_PART), lambda k: (k, 0, 0)), ANY],
        out_specs=(parcel_block, parcel_block),
        scratch_shapes=[pltpu.VMEM((GROUP, OWNED, F_PAD), BF)],
        cost_estimate=SMALL,
        compiler_params=params(24),
    )(index, feedforward_weight, partner)
    feed = exchange_sends(*parcels, (group_tokens, rows))
    feed = exchange_place(feed, index).reshape(GROUP * OWNED, 3 * F_PAD)
    feed_partner = swap(feed, "b")
    w_small = tie(w_small, feed)
    rows = tie(rows, group_tokens)
    rows_left, rows_right = shift(rows, "x", 1), shift(rows, "x", 3)

    token_block = pl.BlockSpec((2, ROWS, D), lambda k: (k, 0, 0))
    small_block = pl.BlockSpec((D, 256), lambda k: (0, 0))
    gains_block = pl.BlockSpec((8, D), lambda k: (0, 0))
    normed_a, raw, gains = pl.pallas_call(
        project,
        grid=(4,),
        out_shape=(
            jax.ShapeDtypeStruct((GROUP, ROWS, D), BF),
            jax.ShapeDtypeStruct((256, 1024), F32),
            jax.ShapeDtypeStruct((8, D), F32),
        ),
        in_specs=[token_block, small_block],
        out_specs=(token_block, pl.BlockSpec((256, 2 * ROWS), lambda k: (0, k)), gains_block),
        cost_estimate=SMALL,
        compiler_params=params(32),
    )(group_tokens, w_small)
    steps = jnp.arange(HEAD_DIM // 2, dtype=F32)
    freqs = jnp.exp(steps * (-2.0 * math.log(10000.0) / HEAD_DIM))
    first = y * 1024

    def turn(frequencies, first, count):
        places = (first + jnp.arange(count, dtype=jnp.int32)).astype(F32)
        angle = frequencies[:, None] * places[None, :]
        return jnp.cos(angle), jnp.sin(angle)

    group_turn = turn(lax.dynamic_slice_in_dim(freqs, PART * j, PART), first, 1024)
    own_turn = turn(freqs, first + ROWS * j, ROWS)
    keys = rotate(raw[Q_PART : Q_PART + 2 * PART].reshape(2, PART, 1024), *group_turn)
    values = raw[Q_PART + 2 * PART : Q_PART + KV_PART].reshape(2, PART, 1024)
    pair = jnp.concatenate([keys, values]).astype(BF).reshape(KV_PART, 1024)
    pair = tie(pair, rows_left, rows_right)
    rows_top, rows_bottom = shift(rows_left[:4], "x", 1), shift(rows_right[4:], "x", 3)
    pair_back = [push(pair, "y", 1), push(pair, "y", 2)]
    q_raw = raw[:Q_PART].astype(BF).reshape(Q_PART, GROUP, ROWS).transpose(1, 0, 2)
    q_raw = exchange(q_raw)
    feed_partner = tie(feed_partner, *pair_back)
    q_raw = q_raw.astype(F32).reshape(LOCAL_HEADS, 2, HEAD_DIM // 2, ROWS)
    queries = rotate(q_raw, *own_turn).astype(BF).reshape(LOCAL_HEADS, HEAD_DIM, ROWS)
    spans = direct(jnp.stack([pair] + pair_back), "x")
    spans[1:] = [tie(span, q_raw, rows_top, rows_bottom) for span in spans[1:]]
    feed_pair = both_in_order(feed, feed_partner, b)
    w_feed = lax.all_gather(feed_pair, "y", axis=1, tiled=True).reshape(D, 3 * F_PAD)
    back_pieces = direct(tie(cotangent, *spans[1:]), "x")
    spans = spans + [swap(piece, "c") for piece in spans]
    rows_top = tie(rows_top, *spans[5:])
    w_output = place_rows([rows, rows_left, rows_right, rows_top, rows_bottom], index)

    width = LOCAL_HEADS * ROWS
    held_spans = [pltpu.VMEM((HEAD_DIM, 3072), BF)] * 2
    probs, attended = pl.pallas_call(
        attend,
        out_shape=(
            jax.ShapeDtypeStruct((TILES, ROWS, width), F32),
            jax.ShapeDtypeStruct((LOCAL_HEADS, HEAD_DIM, ROWS), BF),
        ),
        in_specs=[SMEM, SMEM] + [VMEM] * 9,
        out_specs=(VMEM, VMEM),
        scratch_shapes=[pltpu.VMEM((HEAD_DIM, width), BF)] + held_spans,
        cost_estimate=SMALL,
        compiler_params=params(40),
    )(base, index, queries, *spans)
    attended = attended.reshape(LOCAL_HEADS * HEAD_DIM, ROWS)
    branch = low_bits(dot(attended, w_output, 0, 1))
    back_pieces[1:] = [tie(piece, branch) for piece in back_pieces[1:]]
    other_branch = tie(swap(branch, "t"), *back_pieces[1:])
    residual = inflow + (branch.astype(F32) + other_branch.astype(F32))

    rate_b = rms_rate(residual)
    normed_b = tie((residual * rate_b * gains[1]).astype(BF), w_feed)
    group_b = lax.all_gather(normed_b, ("x", "c"), axis=0).reshape(1024, D)
    group_back = group_place(back_pieces, index).reshape(1024, D)
    d_hidden = tie(dot(group_back, w_feed[:, 2 * F_PAD :], 1, 0), normed_b)
    gate_up = dot(group_b, w_feed[:, : 2 * F_PAD], 1, 0)
    gate, up = gate_up[:, :F_PAD], gate_up[:, F_PAD:]
    root = math.sqrt(2.0 / math.pi)
    bend = jnp.tanh(root * (gate + 0.044715 * gate * gate * gate))
    gelu = 0.5 * gate * (1.0 + bend)
    slope = 0.5 * (1.0 + bend) + 0.5 * gate * (1.0 - bend * bend) * root * (
        1.0 + 3.0 * 0.044715 * gate * gate
    )
    hidden = (gelu * up).astype(BF)
    d_gate_up = jnp.concatenate(
        [(d_hidden * up * slope).astype(BF), (d_hidden * gelu).astype(BF)], axis=1
    )
    normb_part = low_bits(dot(d_gate_up, w_feed[:, : 2 * F_PAD], 1, 1))
    normb_low = lax.psum_scatter(
        normb_part.reshape(GROUP, ROWS, D), ("x", "c"), scatter_dimension=0
    )
    down_grad = dot(tie(group_back, normb_part), hidden, 0, 0).astype(BF)
    gate_grad = dot(tie(group_b, normb_part), d_gate_up, 0, 0).astype(BF)
    feed_part = low_bits(dot(hidden, w_feed[:, 2 * F_PAD :], 1, 1)).reshape(GROUP, ROWS, D)
    normb_low = tie(normb_low, down_grad, gate_grad, feed_part)
    grad_normb = tensor_sum(normb_low)
    feed_grad = jnp.concatenate([gate_grad, down_grad], axis=1).reshape(2, -1, 3 * F_PAD)
    feed_grad = lax.psum_scatter(feed_grad, "y", scatter_dimension=1, tiled=True)
    scaled = grad_normb * gains[1]
    grad_resid = (
        cotangent.astype(F32)
        + rate_b * scaled
        - residual * rate_b**3 * jnp.mean(scaled * residual, axis=-1, keepdims=True)
    )
    gain_b = jnp.sum(grad_normb * residual * rate_b, axis=0)
    resid_low = grad_resid.astype(BF)
    grad_att = dot(w_output, resid_low, 0, 1).astype(BF).reshape(LOCAL_HEADS, HEAD_DIM, ROWS)

    span_parts = jax.ShapeDtypeStruct((4, 3, KV_PART, 1024), BF)
    grad_q, span_mine, span_theirs = pl.pallas_call(
        attend_back,
        out_shape=(
            jax.ShapeDtypeStruct((LOCAL_HEADS, HEAD_DIM, ROWS), F32),
            span_parts,
            span_parts,
        ),
        in_specs=[SMEM, SMEM] + [VMEM] * 11,
        out_specs=(VMEM, VMEM, VMEM),
        scratch_shapes=[
            pltpu.VMEM((HEAD_DIM, width), BF),
            pltpu.VMEM((HEAD_DIM, width), BF),
            pltpu.VMEM((TILES, ROWS, width), F32),
        ]
        + held_spans * 2,
        cost_estimate=SMALL,
        compiler_params=params(44),
    )(base, index, queries, probs, grad_att, *spans)
    query_grad = (
        rotate(grad_q.reshape(LOCAL_HEADS, 2, HEAD_DIM // 2, ROWS), own_turn[0], -own_turn[1])
        .astype(BF)
        .reshape(GROUP, Q_PART, ROWS)
    )
    moved = jnp.concatenate([query_grad, attended.reshape(GROUP, Q_PART, ROWS)], axis=1)
    back_terms = scatter_terms(span_mine, span_theirs, "c", "x", index)
    moved = exchange(tie(moved, back_terms[0])).transpose(1, 0, 2).reshape(2 * Q_PART, 1024)
    query_grad, group_attended = moved[:Q_PART], moved[Q_PART:]
    back_terms[1] = tie(back_terms[1], moved)
    back = total_of(back_terms)
    back = (
        back[0]
        + push(back[1].astype(BF), "y", -1).astype(F32)
        + push(back[2].astype(BF), "y", -2).astype(F32)
    )
    grad_k = rotate(back[: 2 * PART].reshape(2, PART, 1024), group_turn[0], -group_turn[1])
    grad_v = back[2 * PART :].reshape(2, PART, 1024)
    pair_grad = jnp.concatenate([grad_k, grad_v]).astype(BF).reshape(KV_PART, 1024)

    sent = jnp.concatenate([query_grad, pair_grad])
    feed_grad = tie(feed_grad, sent)
    group_resid = lax.all_gather(tie(resid_low, feed_grad), ("x", "c"), axis=0)
    feed_grad = pair_total(feed_grad, 0, b, "b").astype(BF)
    side = jax.ShapeDtypeStruct((4, ROWS, D), BF)
    side_block = pl.BlockSpec((1, ROWS, D), lambda k: (k, 0, 0))
    norma_mine, norma_theirs, gain_a = pl.pallas_call(
        project_back,
        grid=(4,),
        out_shape=(side, side, jax.ShapeDtypeStruct((8, D), F32)),
        in_specs=[
            SMEM,
            pl.BlockSpec((Q_PART + KV_PART, 2 * ROWS), lambda k: (0, k)),
            small_block,
            token_block,
        ],
        out_specs=(side_block, side_block, gains_block),
        scratch_shapes=[pltpu.VMEM((2, ROWS, D), BF)],
        cost_estimate=SMALL,
        compiler_params=params(32),
    )(index, sent, w_small, group_tokens)
    rate_a = rms_rate(inflow)
    norma_terms = scatter_terms(norma_mine, norma_theirs, "c", "x", index)
    extra = jnp.concatenate([gain_a[:1], 0.5 * gain_b[None], jnp.zeros((6, D), F32)])
    parts = grads_by_chunk(
        normed_a, sent, extra, group_resid, group_attended, index, norma_terms[0]
    )
    norma_terms[1:] = [tie(term, parts[0]) for term in norma_terms[1:]]
    norma_low = low_bits(total_of(norma_terms))
    out_low = lax.psum_scatter(tie(feed_part, parts[0]), ("x", "c"), scatter_dimension=0)
    late = jnp.concatenate([feed_grad, row_scatter(parts, b)], axis=1)
    late = exchange(late.reshape(GROUP, OWNED, 3 * F_PAD + 512))
    small_grad = late[:, :, 3 * F_PAD : 3 * F_PAD + 256]
    other_out = swap(out_low, "t")
    out_tokens = (residual + (out_low.astype(F32) + other_out.astype(F32))).astype(BF)
    grad_norma = tensor_sum(norma_low)
    scaled = grad_norma * gains[0]
    input_grad = (
        grad_resid
        + rate_a * scaled
        - inflow * rate_a**3 * jnp.mean(scaled * inflow, axis=-1, keepdims=True)
    )


    def update(grads, weight, moment, second, part, start, rate, pair=False):
        return pl.pallas_call(
            adam_columns(part, start, rate, pair),
            out_shape=(jax.ShapeDtypeStruct(weight.shape, F32),) * 3,
            in_specs=[VMEM] * (3 + len(grads)),
            out_specs=(VMEM,) * 3,
            cost_estimate=SMALL,
            compiler_params=params(32),
        )(*grads, weight, moment, second)

    other_grad = swap(tie(small_grad, other_out), "t")
    query_new = update(
        [late], query_weight, query_moment, query_second, Q_PART, 3 * F_PAD, wide_rate
    )
    pair_new = update(
        [small_grad, other_grad],
        keyvalue_weight,
        keyvalue_moment,
        keyvalue_second,
        KV_PART,
        Q_PART,
        wide_rate,
        True,
    )
    output_new = update(
        [late], output_weight, output_moment, output_second, Q_PART, 3 * F_PAD + 256, output_rate
    )
    matrix = pl.BlockSpec((1, OWNED, 8 * F_PART), lambda k: (k, 0, 0))
    feed_new = pl.pallas_call(
        adam_columns(F_PART, 0, wide_rate),
        grid=(3,),
        out_shape=(jax.ShapeDtypeStruct(feedforward_weight.shape, F32),) * 3,
        in_specs=[pl.BlockSpec((GROUP, OWNED, F_PAD), lambda k: (0, 0, k))] + [matrix] * 3,
        out_specs=(matrix,) * 3,
        cost_estimate=SMALL,
        compiler_params=params(32),
    )(late, feedforward_weight, feedforward_moment, feedforward_second)
    gain_grad = small_grad.astype(F32) + other_grad.astype(F32)
    gain_grad = jnp.sum(gain_grad[:, :, Q_PART + KV_PART : Q_PART + KV_PART + 2], axis=0).T
    gains_new = adam(norm_gains, gain_grad, gains_moment, gains_second, 0.3, 0.0)
    return (
        out_tokens,
        input_grad,
        *query_new,
        *pair_new,
        *output_new,
        *feed_new,
        *gains_new,
    )


def solution(mesh):
    grid = Mesh(mesh.devices.reshape(2, 4, 4, 2, 2), ("b", "y", "x", "c", "t"))
    rows = ("b", "y", "x", "c")
    token = P(rows, None)
    split = P(rows, "t")
    whole = P(rows, None)
    feed = P(None, rows, "t")
    gain = P(None, rows)
    weights = (split,) * 3 + (whole,) * 3 + (split,) * 3 + (feed,) * 3 + (gain,) * 3
    return jax.shard_map(
        local,
        mesh=grid,
        in_specs=(token, token) + weights,
        out_specs=(token, token) + weights,
        check_vma=False,
    )
```

```python
import math

import jax
import jax.numpy as jnp
from jax import lax
from jax.experimental import pallas as pl
from jax.experimental.pallas import tpu as pltpu
from jax.sharding import Mesh
from jax.sharding import PartitionSpec as P

D = 2560
HEADS = 10
HEAD_DIM = 256
STEP = 10
ROWS = 128
GROUP = 8
OWNED = 40
Q_PART = 160
KV_PART = 64
F_PART = 480
F_PAD = 512
LOCAL_HEADS = 5
TILES = 17
BF = jnp.bfloat16
F32 = jnp.float32
ANY = pl.BlockSpec(memory_space=pl.ANY)
SMEM = pl.BlockSpec(memory_space=pltpu.SMEM)
VMEM = pl.BlockSpec(memory_space=pltpu.VMEM)


SMALL = pl.CostEstimate(flops=1, transcendentals=0, bytes_accessed=1)


def params(mib):
    return pltpu.CompilerParams(vmem_limit_bytes=mib * 1024 * 1024)


def dot(left, right, left_dim, right_dim):
    return lax.dot_general(
        left, right, (((left_dim,), (right_dim,)), ((), ())), preferred_element_type=F32
    )


def shift(value, axis, step):
    return lax.ppermute(value, axis, [(i, (i + step) % 4) for i in range(4)])


def push(value, axis, step):
    return lax.ppermute(value, axis, [(i, i + step) for i in range(4) if 0 <= i + step < 4])


def swap(value, axis):
    return lax.ppermute(value, axis, [(0, 1), (1, 0)])


STEPS = (0, 1, 3, 2)
Y_AT, X_AT, B_AT, C_AT = 0, 4, 8, 10


def tie(value, *others):
    def body(*refs):
        del refs

    return pl.pallas_call(
        body,
        out_shape=jax.ShapeDtypeStruct(value.shape, value.dtype),
        in_specs=[ANY] * (1 + len(others)),
        out_specs=ANY,
        input_output_aliases={0: 0},
        cost_estimate=SMALL,
    )(value, *others)


def place(pieces, index, shape, target):
    count = len(pieces)

    def body(index_ref, *refs):
        out, sems = refs[count], refs[count + 1]
        copies = [
            pltpu.make_async_copy(refs[k], target(out, index_ref, k), sems.at[k])
            for k in range(count)
        ]
        for copy in copies:
            copy.start()
        for copy in copies:
            copy.wait()

    return pl.pallas_call(
        body,
        out_shape=jax.ShapeDtypeStruct(shape, pieces[0].dtype),
        in_specs=[SMEM] + [VMEM] * count,
        out_specs=ANY,
        scratch_shapes=[pltpu.SemaphoreType.DMA((count,))],
        cost_estimate=SMALL,
        compiler_params=params(24),
    )(index, *pieces)


def direct(value, axis):
    return [value] + [shift(value, axis, step) for step in STEPS[1:]]


def group_place(mine, index):
    pieces = mine + [swap(piece, "c") for piece in mine]

    def target(out, index_ref, k):
        return out.at[2 * index_ref[X_AT + k % 4] + index_ref[C_AT + k // 4]]

    return place(pieces, index, (GROUP,) + mine[0].shape, target)


def group_gather(value, index):
    return group_place(direct(value, "x"), index)


def two_step_gather(value, index):
    half = value.shape[0] // 2
    left, right = shift(value, "x", 1), shift(value, "x", 3)
    top, bottom = shift(left[:half], "x", 1), shift(right[half:], "x", 3)
    mine = [value, left, right, top, bottom]
    pieces = mine + [swap(piece, "c") for piece in mine]
    pieces = [
        piece if k % 5 > 2 else piece.reshape((2, half) + value.shape[1:])
        for k, piece in enumerate(pieces)
    ]

    def target(out, index_ref, k):
        spot = 2 * index_ref[X_AT + min(k % 5, 3)] + index_ref[C_AT + k // 5]
        return out.at[spot] if k % 5 < 3 else out.at[spot, k % 5 - 3]

    out = place(pieces, index, (GROUP, 2, half) + value.shape[1:], target)
    return out.reshape((GROUP,) + value.shape), (left, right)


def place_rows(mine, index):
    pieces = mine + [swap(piece, "c") for piece in mine]

    def target(out, index_ref, k):
        spot = 2 * index_ref[X_AT + min(k % 5, 3)] + index_ref[C_AT + k // 5]
        if k % 5 < 3:
            return out.at[:, spot]
        return out.at[pl.ds((k % 5 - 3) * 4, 4), spot]

    width = mine[0].shape[2]
    return place(pieces, index, (8, GROUP, OWNED, width), target).reshape(D, width)


def pair_gather(mine, theirs, pair_axis, ring_axis, index, after=()):
    pieces = direct(jnp.stack([mine, theirs]), ring_axis)
    ring_at, pair_at = (X_AT, C_AT) if ring_axis == "x" else (Y_AT, B_AT)

    def body(index_ref, *refs):
        out, sems = refs[-2:]
        copies = []
        for k in range(4):
            for h in range(2):
                spot, side = index_ref[ring_at + k], index_ref[pair_at + h]
                to = out.at[spot, side] if ring_axis == "x" else out.at[side, spot]
                copies.append(pltpu.make_async_copy(refs[k].at[h], to, sems.at[2 * k + h]))
        for copy in copies:
            copy.start()
        for copy in copies:
            copy.wait()

    shape = ((4, 2) if ring_axis == "x" else (2, 4)) + mine.shape
    return pl.pallas_call(
        body,
        out_shape=jax.ShapeDtypeStruct(shape, mine.dtype),
        in_specs=[SMEM] + [VMEM] * 4 + [ANY] * len(after),
        out_specs=ANY,
        scratch_shapes=[pltpu.SemaphoreType.DMA((8,))],
        cost_estimate=SMALL,
        compiler_params=params(16),
    )(index, *pieces, *after)


def exchange_sends(mine, theirs, after=()):
    pair = jnp.stack([mine, swap(theirs, "c")], axis=1)
    if after:
        pair = tie(pair, *after)
    return [pair[0]] + [shift(pair[k], "x", STEPS[k]) for k in range(1, 4)]


def exchange_place(pieces, index):
    def body(index_ref, *refs):
        out, sems = refs[-2:]
        copies = []
        for k in range(4):
            for h in range(2):
                to = out.at[index_ref[X_AT + k], index_ref[C_AT + h]]
                copies.append(pltpu.make_async_copy(refs[k].at[h], to, sems.at[2 * k + h]))
        for copy in copies:
            copy.start()
        for copy in copies:
            copy.wait()

    return pl.pallas_call(
        body,
        out_shape=jax.ShapeDtypeStruct((4, 2) + pieces[0].shape[1:], pieces[0].dtype),
        in_specs=[SMEM] + [VMEM] * 4,
        out_specs=ANY,
        scratch_shapes=[pltpu.SemaphoreType.DMA((8,))],
        cost_estimate=SMALL,
        compiler_params=params(16),
    )(index, *pieces)


def group_exchange(mine, theirs, index):
    return exchange_place(exchange_sends(mine, theirs), index)


def fold(mine, received, index, at, after=()):
    shape = mine.shape[1:]

    def body(index_ref, mine_ref, received_ref, *refs):
        for k, out in enumerate(refs[len(after) :]):
            spot = index_ref[at + (0, 2, 1, 3)[k]]
            total = mine_ref[spot].astype(F32) + received_ref[spot].astype(F32)
            out[...] = total.astype(out.dtype)

    return pl.pallas_call(
        body,
        out_shape=(jax.ShapeDtypeStruct(shape, F32),) + (jax.ShapeDtypeStruct(shape, BF),) * 3,
        in_specs=[SMEM, VMEM, VMEM] + [ANY] * len(after),
        out_specs=(VMEM,) * 4,
        cost_estimate=SMALL,
        compiler_params=params(40),
    )(index, mine, received, *after)


def scatter_terms(mine, theirs, pair_axis, ring_axis, index, after=()):
    at = X_AT if ring_axis == "x" else Y_AT
    own, *others = fold(mine, swap(theirs, pair_axis), index, at, after)
    return [own] + [shift(other, ring_axis, step) for step, other in zip(STEPS[1:], others)]


def total_of(terms):
    return sum(term.astype(F32) for term in terms)


def scatter(*args, **kwargs):
    return total_of(scatter_terms(*args, **kwargs))


def pair_total(parts, axis, place_at, pair_axis):
    mine, theirs = sides(parts, axis, place_at)
    return mine.astype(F32) + swap(theirs, pair_axis).astype(F32)


def sides(parts, axis, place_at):
    return (
        lax.dynamic_index_in_dim(parts, place_at, axis, keepdims=False),
        lax.dynamic_index_in_dim(parts, 1 - place_at, axis, keepdims=False),
    )


def both_in_order(mine, theirs, place_at):
    first = place_at == 0
    return jnp.stack([jnp.where(first, mine, theirs), jnp.where(first, theirs, mine)])


def low_bits(value):
    return lax.optimization_barrier(value.astype(BF))


def tensor_sum(low):
    return low.astype(F32) + swap(low, "t").astype(F32)


def exchange(value):
    return lax.all_to_all(value, ("x", "c"), split_axis=0, concat_axis=0, tiled=True)


def hand_out(index_ref, held, mine_ref, theirs_ref):
    for k in range(4):
        spot = 2 * index_ref[X_AT + (0, 2, 1, 3)[k]]
        mine_ref[k] = held[spot + index_ref[C_AT]]
        theirs_ref[k] = held[spot + index_ref[C_AT + 1]]


def pack_small(index_ref, q_ref, kv_ref, gain_ref, mine_ref, theirs_ref, held):
    rest = jnp.zeros((OWNED, 256 - Q_PART - KV_PART - 2), F32)
    half, part = HEAD_DIM // 2, KV_PART // 4
    for j in range(GROUP):
        held[j] = jnp.concatenate(
            [
                q_ref[:, Q_PART * j : Q_PART * (j + 1)],
                kv_ref[:, part * j : part * (j + 1)],
                kv_ref[:, half + part * j : half + part * (j + 1)],
                kv_ref[:, 2 * half + 2 * part * j : 2 * half + 2 * part * (j + 1)],
                gain_ref[...],
                rest,
            ],
            axis=1,
        ).astype(BF)
    hand_out(index_ref, held, mine_ref, theirs_ref)


def pack_feed(index_ref, w_ref, after_ref, mine_ref, theirs_ref, held):
    del after_ref
    rest = jnp.zeros((OWNED, F_PAD - F_PART), F32)
    for j in range(GROUP):
        held[j] = jnp.concatenate(
            [w_ref[0, :, F_PART * j : F_PART * (j + 1)], rest], axis=1
        ).astype(BF)
    hand_out(index_ref, held, mine_ref, theirs_ref)


def adam(weight, grad, moment, second, rate, decay):
    moment_new = 0.9 * moment + 0.1 * grad
    second_new = 0.95 * second + 0.05 * grad * grad
    ratio = moment_new / (1.0 - 0.9**STEP) / (jnp.sqrt(second_new / (1.0 - 0.95**STEP)) + 1e-08)
    return (moment_new, second_new, weight - rate * (ratio + decay * weight))


def adam_columns(part, start, rate, pair=False):
    if pair:
        cuts = [(start, PART), (start + PART, PART), (start + 2 * PART, 2 * PART)]
    else:
        cuts = [(start, part)]

    def body(*refs):
        *g_refs, w_ref, m_ref, v_ref, mo_ref, vo_ref, wo_ref = refs
        grad = sum(
            jnp.concatenate(
                [
                    g_ref[j, :, at : at + count].astype(F32)
                    for at, count in cuts
                    for j in range(GROUP)
                ],
                axis=1,
            )
            for g_ref in g_refs
        )
        index = (0,) if len(w_ref.shape) == 3 else (slice(None),)
        m, v, w = adam(w_ref[index], grad, m_ref[index], v_ref[index], rate, 0.1)
        mo_ref[index] = m
        vo_ref[index] = v
        wo_ref[index] = w

    return body


def window(base_ref, i):
    start = pl.multiple_of(ROWS * (base_ref[1] + i), ROWS)
    return pl.ds(start, ROWS), base_ref[0] * 8 + base_ref[1] + i >= 16


PART = HEAD_DIM // 16


def head_rows(j):
    return (
        (slice(2 * PART * j, 2 * PART * j + PART), slice(PART * j, PART * j + PART)),
        (
            slice(2 * PART * j + PART, 2 * PART * (j + 1)),
            slice(HEAD_DIM // 2 + PART * j, HEAD_DIM // 2 + PART * (j + 1)),
        ),
    )


def hold_spans(index_ref, pieces, keys, values):
    for k, piece in enumerate(pieces):
        spot = 2 * index_ref[X_AT + k % 4] + index_ref[C_AT + k // 4]
        rows = pl.ds(pl.multiple_of(2 * PART * spot, 2 * PART), 2 * PART)
        for back in range(3):
            lanes = slice(1024 * (2 - back), 1024 * (3 - back))
            keys[rows, lanes] = piece[back, : 2 * PART]
            values[rows, lanes] = piece[back, 2 * PART :]


def hold_queries(q_ref, qs):
    for h in range(LOCAL_HEADS):
        for j in range(GROUP):
            for to, at in head_rows(j):
                qs[to, ROWS * h : ROWS * (h + 1)] = q_ref[h, at]


def attend(base_ref, index_ref, q_ref, *refs):
    pieces, (p_ref, a_ref, qs, keys, values) = refs[:GROUP], refs[GROUP:]
    hold_spans(index_ref, pieces, keys, values)
    hold_queries(q_ref, qs)
    width = LOCAL_HEADS * ROWS
    key_at = lax.broadcasted_iota(jnp.int32, (ROWS, width), 0)
    query_at = lax.broadcasted_iota(jnp.int32, (ROWS, width), 1) % ROWS
    top = jnp.full((1, width), -1e30, F32)
    for i in range(TILES):
        lanes, exists = window(base_ref, i)
        scores = dot(keys[:, lanes], qs[...], 0, 0) * (HEAD_DIM**-0.5)
        if i == 0:
            scores = jnp.where((key_at > query_at) & exists, scores, -1e30)
        elif i == TILES - 1:
            scores = jnp.where(key_at <= query_at, scores, -1e30)
        else:
            scores = jnp.where(exists, scores, -1e30)
        p_ref[i] = scores
        top = jnp.maximum(top, jnp.max(scores, axis=0, keepdims=True))
    total = jnp.zeros((1, width), F32)
    for i in range(TILES):
        weights = jnp.exp(p_ref[i] - top)
        p_ref[i] = weights
        total = total + jnp.sum(weights, axis=0, keepdims=True)
    scale = 1.0 / total
    result = jnp.zeros((HEAD_DIM, width), F32)
    for i in range(TILES):
        lanes, _ = window(base_ref, i)
        probs = p_ref[i] * scale
        p_ref[i] = probs
        result = result + dot(values[:, lanes], probs.astype(BF), 1, 0)
    for h in range(LOCAL_HEADS):
        a_ref[h] = result[:, ROWS * h : ROWS * (h + 1)].astype(BF)


def attend_back(base_ref, index_ref, q_ref, p_ref, da_ref, *refs):
    pieces = refs[:GROUP]
    dq_ref, mine_ref, theirs_ref, qs, das, dps, keys, values, d_keys, d_values = refs[-10:]
    hold_spans(index_ref, pieces, keys, values)
    hold_queries(q_ref, qs)
    width = LOCAL_HEADS * ROWS
    for h in range(LOCAL_HEADS):
        das[:, ROWS * h : ROWS * (h + 1)] = da_ref[h]
    d_keys[...] = jnp.zeros(d_keys.shape, BF)
    d_values[...] = jnp.zeros(d_values.shape, BF)
    delta = jnp.zeros((1, width), F32)
    for i in range(TILES):
        lanes, _ = window(base_ref, i)
        probs = p_ref[i]
        d_probs = dot(values[:, lanes], das[...], 0, 0)
        dps[i] = d_probs
        delta = delta + jnp.sum(probs * d_probs, axis=0, keepdims=True)
        d_values[:, lanes] = dot(das[...], probs.astype(BF), 1, 1).astype(BF)
    dq = jnp.zeros((HEAD_DIM, width), F32)
    for i in range(TILES):
        lanes, _ = window(base_ref, i)
        d_scores = (p_ref[i] * (dps[i] - delta)).astype(BF)
        dq = dq + dot(keys[:, lanes], d_scores, 1, 0)
        d_keys[:, lanes] = (dot(qs[...], d_scores, 1, 1) * (HEAD_DIM**-0.5)).astype(BF)
    for h in range(LOCAL_HEADS):
        for j in range(GROUP):
            for at, to in head_rows(j):
                dq_ref[h, to] = dq[at, ROWS * h : ROWS * (h + 1)] * (HEAD_DIM**-0.5)
    core = base_ref[1] % 2
    for j in range(GROUP):
        rows = slice(2 * PART * j, 2 * PART * (j + 1))
        for ref, match in ((mine_ref, j % 2), (theirs_ref, 1 - j % 2)):

            @pl.when(core == match)
            def _(ref=ref, rows=rows, j=j):
                for back in range(3):
                    lanes = slice(1024 * (2 - back), 1024 * (3 - back))
                    ref[j // 2, back, : 2 * PART] = d_keys[rows, lanes]
                    ref[j // 2, back, 2 * PART :] = d_values[rows, lanes]


def project(x_ref, w_ref, n_ref, raw_ref, gains_ref):
    @pl.when(pl.program_id(0) == 0)
    def _():
        turned = w_ref[:, 128:].astype(F32).T
        at = Q_PART + KV_PART - 128
        gains_ref[...] = turned[at : at + 8]

    x = x_ref[...].reshape(2 * ROWS, D).astype(F32)
    normed = (x * rms_rate(x) * gains_ref[0:1]).astype(BF)
    n_ref[...] = normed.reshape(2, ROWS, D)
    raw_ref[...] = dot(normed, w_ref[...], 1, 0).T


def project_back(index_ref, sent_ref, w_ref, x_ref, mine_ref, theirs_ref, gain_ref, held):
    @pl.when(pl.program_id(0) == 0)
    def _():
        gain_ref[...] = jnp.zeros(gain_ref.shape, F32)

    sent = sent_ref[...].astype(F32).T.astype(BF)
    part = dot(sent, w_ref[:, : Q_PART + KV_PART], 1, 1)
    x = x_ref[...].reshape(2 * ROWS, D).astype(F32)
    gain_ref[0:1] += jnp.sum(part * x * rms_rate(x), axis=0, keepdims=True)
    held[...] = part.astype(BF).reshape(2, ROWS, D)
    mine_ref[0] = held[index_ref[C_AT]]
    theirs_ref[0] = held[index_ref[C_AT + 1]]


def chunk_grads(index_ref, rows_ref, cols_ref, extra_ref, rows2_ref, cols2_ref, after_ref, *refs):
    del after_ref
    *out_refs, total, held = refs
    step, part, part2 = pl.program_id(0), cols_ref.shape[0], cols2_ref.shape[0]

    @pl.when(step == 0)
    def _():
        total[...] = jnp.zeros(total.shape, F32)
        total[part : part + 8] = extra_ref[...]

    @pl.when(step < 4)
    def _():
        total[:part] += dot(cols_ref[...], rows_ref[...].reshape(2 * ROWS, D), 1, 0)

    @pl.when(step >= 4)
    def _():
        rows = rows2_ref[...].reshape(2 * ROWS, D)
        total[256 : 256 + part2] += dot(cols2_ref[...], rows, 1, 0)

    @pl.when(step == 7)
    def _():
        block, whole = GROUP * OWNED, total[...].T
        for k in range(8):
            held[k % 4, k // 4] = whole[k * block : (k + 1) * block].astype(BF)
        for k, out in enumerate(out_refs):
            out[...] = held[index_ref[Y_AT + (0, 2, 1, 3)[k]]]


def grads_by_chunk(rows, cols, extra, rows2, cols2, index, after):
    shape = (2, GROUP * OWNED, 512)

    def first(k):
        return jnp.minimum(k, 3)

    def second(k):
        return jnp.maximum(k - 4, 0)

    return pl.pallas_call(
        chunk_grads,
        grid=(8,),
        out_shape=(jax.ShapeDtypeStruct(shape, BF),) * 4,
        in_specs=[
            SMEM,
            pl.BlockSpec((2, ROWS, D), lambda k: (first(k), 0, 0)),
            pl.BlockSpec((cols.shape[0], 2 * ROWS), lambda k: (0, first(k))),
            pl.BlockSpec((8, D), lambda k: (0, 0)),
            pl.BlockSpec((2, ROWS, D), lambda k: (second(k), 0, 0)),
            pl.BlockSpec((cols2.shape[0], 2 * ROWS), lambda k: (0, second(k))),
            ANY,
        ],
        out_specs=(pl.BlockSpec(shape, lambda k: (0, 0, 0)),) * 4,
        scratch_shapes=[
            pltpu.VMEM((512, D), F32),
            pltpu.VMEM((4, 2, GROUP * OWNED, 512), BF),
        ],
        cost_estimate=SMALL,
        compiler_params=params(40),
    )(index, rows, cols, extra, rows2, cols2, after)


def along_y(parts):
    return [parts[0]] + [shift(part, "y", step) for step, part in zip(STEPS[1:], parts[1:])]


def rms_rate(values):
    return lax.rsqrt(jnp.mean(values * values, axis=-1, keepdims=True) + 1e-06)


def rotate(values, cosine, sine):
    first, second = values[..., 0, :, :], values[..., 1, :, :]
    return jnp.stack([first * cosine - second * sine, second * cosine + first * sine], axis=-3)


def local(
    tokens,
    cotangent,
    query_weight,
    query_moment,
    query_second,
    keyvalue_weight,
    keyvalue_moment,
    keyvalue_second,
    output_weight,
    output_moment,
    output_second,
    feedforward_weight,
    feedforward_moment,
    feedforward_second,
    norm_gains,
    gains_moment,
    gains_second,
):
    x, y, c, b = (lax.axis_index(name) for name in "xycb")
    j = 2 * x + c
    wide_rate = 1.5 * D**-0.5
    output_rate = 1.5 * (HEADS * HEAD_DIM // 32) ** -0.5
    index = jnp.stack(
        [(y + 4 - step) % 4 for step in STEPS] + [(x + 4 - step) % 4 for step in STEPS]
        + [b, 1 - b, c, 1 - c]
    ).astype(jnp.int32)
    base = jnp.stack([y, j]).astype(jnp.int32)

    inflow = tokens.astype(F32)
    parcel = jax.ShapeDtypeStruct((4, OWNED, 256), BF)
    parcels = pl.pallas_call(
        pack_small,
        out_shape=(parcel, parcel),
        in_specs=[SMEM] + [VMEM] * 3,
        out_specs=(VMEM, VMEM),
        scratch_shapes=[pltpu.VMEM((GROUP, OWNED, 256), BF)],
        cost_estimate=SMALL,
        compiler_params=params(16),
    )(index, query_weight, keyvalue_weight, norm_gains.T)
    small = group_exchange(*parcels, index).reshape(GROUP * OWNED, 256)
    group_tokens = lax.all_gather(tie(tokens, small), ("x", "c"), axis=0)
    partner = swap(small, "b")
    w_small = pair_gather(small, partner, "b", "y", index).reshape(D, 256)
    rows = tie(output_weight.astype(BF), w_small)
    rows = pair_gather(rows, swap(rows, "b"), "b", "y", index).reshape(8, OWNED, -1)
    parcel = jax.ShapeDtypeStruct((4, OWNED, 3 * F_PAD), BF)
    parcel_block = pl.BlockSpec((4, OWNED, F_PAD), lambda k: (0, 0, k))
    parcels = pl.pallas_call(
        pack_feed,
        grid=(3,),
        out_shape=(parcel, parcel),
        in_specs=[SMEM, pl.BlockSpec((1, OWNED, 8 * F_PART), lambda k: (k, 0, 0)), ANY],
        out_specs=(parcel_block, parcel_block),
        scratch_shapes=[pltpu.VMEM((GROUP, OWNED, F_PAD), BF)],
        cost_estimate=SMALL,
        compiler_params=params(24),
    )(index, feedforward_weight, partner)
    feed = exchange_sends(*parcels, (group_tokens, rows))
    feed = exchange_place(feed, index).reshape(GROUP * OWNED, 3 * F_PAD)
    feed_partner = swap(feed, "b")
    w_small = tie(w_small, feed)
    rows = tie(rows, group_tokens)
    rows_left, rows_right = shift(rows, "x", 1), shift(rows, "x", 3)

    token_block = pl.BlockSpec((2, ROWS, D), lambda k: (k, 0, 0))
    small_block = pl.BlockSpec((D, 256), lambda k: (0, 0))
    gains_block = pl.BlockSpec((8, D), lambda k: (0, 0))
    normed_a, raw, gains = pl.pallas_call(
        project,
        grid=(4,),
        out_shape=(
            jax.ShapeDtypeStruct((GROUP, ROWS, D), BF),
            jax.ShapeDtypeStruct((256, 1024), F32),
            jax.ShapeDtypeStruct((8, D), F32),
        ),
        in_specs=[token_block, small_block],
        out_specs=(token_block, pl.BlockSpec((256, 2 * ROWS), lambda k: (0, k)), gains_block),
        cost_estimate=SMALL,
        compiler_params=params(32),
    )(group_tokens, w_small)
    steps = jnp.arange(HEAD_DIM // 2, dtype=F32)
    freqs = jnp.exp(steps * (-2.0 * math.log(10000.0) / HEAD_DIM))
    first = y * 1024

    def turn(frequencies, first, count):
        places = (first + jnp.arange(count, dtype=jnp.int32)).astype(F32)
        angle = frequencies[:, None] * places[None, :]
        return jnp.cos(angle), jnp.sin(angle)

    group_turn = turn(lax.dynamic_slice_in_dim(freqs, PART * j, PART), first, 1024)
    own_turn = turn(freqs, first + ROWS * j, ROWS)
    keys = rotate(raw[Q_PART : Q_PART + 2 * PART].reshape(2, PART, 1024), *group_turn)
    values = raw[Q_PART + 2 * PART : Q_PART + KV_PART].reshape(2, PART, 1024)
    pair = jnp.concatenate([keys, values]).astype(BF).reshape(KV_PART, 1024)
    pair = tie(pair, rows_left, rows_right)
    rows_top, rows_bottom = shift(rows_left[:4], "x", 1), shift(rows_right[4:], "x", 3)
    pair_back = [push(pair, "y", 1), push(pair, "y", 2)]
    q_raw = raw[:Q_PART].astype(BF).reshape(Q_PART, GROUP, ROWS).transpose(1, 0, 2)
    q_raw = exchange(q_raw)
    feed_partner = tie(feed_partner, *pair_back)
    q_raw = q_raw.astype(F32).reshape(LOCAL_HEADS, 2, HEAD_DIM // 2, ROWS)
    queries = rotate(q_raw, *own_turn).astype(BF).reshape(LOCAL_HEADS, HEAD_DIM, ROWS)
    spans = direct(jnp.stack([pair] + pair_back), "x")
    spans[1:] = [tie(span, q_raw, rows_top, rows_bottom) for span in spans[1:]]
    feed_pair = both_in_order(feed, feed_partner, b)
    w_feed = lax.all_gather(feed_pair, "y", axis=1, tiled=True).reshape(D, 3 * F_PAD)
    back_pieces = direct(tie(cotangent, *spans[1:]), "x")
    spans = spans + [swap(piece, "c") for piece in spans]
    rows_top = tie(rows_top, *spans[5:])
    w_output = place_rows([rows, rows_left, rows_right, rows_top, rows_bottom], index)

    width = LOCAL_HEADS * ROWS
    held_spans = [pltpu.VMEM((HEAD_DIM, 3072), BF)] * 2
    probs, attended = pl.pallas_call(
        attend,
        out_shape=(
            jax.ShapeDtypeStruct((TILES, ROWS, width), F32),
            jax.ShapeDtypeStruct((LOCAL_HEADS, HEAD_DIM, ROWS), BF),
        ),
        in_specs=[SMEM, SMEM] + [VMEM] * 9,
        out_specs=(VMEM, VMEM),
        scratch_shapes=[pltpu.VMEM((HEAD_DIM, width), BF)] + held_spans,
        cost_estimate=SMALL,
        compiler_params=params(40),
    )(base, index, queries, *spans)
    attended = attended.reshape(LOCAL_HEADS * HEAD_DIM, ROWS)
    branch = low_bits(dot(attended, w_output, 0, 1))
    back_pieces[1:] = [tie(piece, branch) for piece in back_pieces[1:]]
    other_branch = tie(swap(branch, "t"), *back_pieces[1:])
    residual = inflow + (branch.astype(F32) + other_branch.astype(F32))

    rate_b = rms_rate(residual)
    normed_b = tie((residual * rate_b * gains[1]).astype(BF), w_feed)
    group_b = lax.all_gather(normed_b, ("x", "c"), axis=0).reshape(1024, D)
    group_back = group_place(back_pieces, index).reshape(1024, D)
    d_hidden = tie(dot(group_back, w_feed[:, 2 * F_PAD :], 1, 0), normed_b)
    gate_up = dot(group_b, w_feed[:, : 2 * F_PAD], 1, 0)
    gate, up = gate_up[:, :F_PAD], gate_up[:, F_PAD:]
    root = math.sqrt(2.0 / math.pi)
    bend = jnp.tanh(root * (gate + 0.044715 * gate * gate * gate))
    gelu = 0.5 * gate * (1.0 + bend)
    slope = 0.5 * (1.0 + bend) + 0.5 * gate * (1.0 - bend * bend) * root * (
        1.0 + 3.0 * 0.044715 * gate * gate
    )
    hidden = (gelu * up).astype(BF)
    d_gate_up = jnp.concatenate(
        [(d_hidden * up * slope).astype(BF), (d_hidden * gelu).astype(BF)], axis=1
    )
    normb_part = low_bits(dot(d_gate_up, w_feed[:, : 2 * F_PAD], 1, 1))
    normb_low = lax.psum_scatter(
        normb_part.reshape(GROUP, ROWS, D), ("x", "c"), scatter_dimension=0
    )
    down_grad = dot(tie(group_back, normb_part), hidden, 0, 0).astype(BF)
    gate_grad = dot(tie(group_b, normb_part), d_gate_up, 0, 0).astype(BF)
    feed_part = low_bits(dot(hidden, w_feed[:, 2 * F_PAD :], 1, 1)).reshape(GROUP, ROWS, D)
    normb_low = tie(normb_low, down_grad, gate_grad, feed_part)
    grad_normb = tensor_sum(normb_low)
    feed_grad = jnp.concatenate([gate_grad, down_grad], axis=1).reshape(2, -1, 3 * F_PAD)
    feed_grad = lax.psum_scatter(feed_grad, "y", scatter_dimension=1, tiled=True)
    scaled = grad_normb * gains[1]
    grad_resid = (
        cotangent.astype(F32)
        + rate_b * scaled
        - residual * rate_b**3 * jnp.mean(scaled * residual, axis=-1, keepdims=True)
    )
    gain_b = jnp.sum(grad_normb * residual * rate_b, axis=0)
    resid_low = grad_resid.astype(BF)
    grad_att = dot(w_output, resid_low, 0, 1).astype(BF).reshape(LOCAL_HEADS, HEAD_DIM, ROWS)

    span_parts = jax.ShapeDtypeStruct((4, 3, KV_PART, 1024), BF)
    grad_q, span_mine, span_theirs = pl.pallas_call(
        attend_back,
        out_shape=(
            jax.ShapeDtypeStruct((LOCAL_HEADS, HEAD_DIM, ROWS), F32),
            span_parts,
            span_parts,
        ),
        in_specs=[SMEM, SMEM] + [VMEM] * 11,
        out_specs=(VMEM, VMEM, VMEM),
        scratch_shapes=[
            pltpu.VMEM((HEAD_DIM, width), BF),
            pltpu.VMEM((HEAD_DIM, width), BF),
            pltpu.VMEM((TILES, ROWS, width), F32),
        ]
        + held_spans * 2,
        cost_estimate=SMALL,
        compiler_params=params(44),
    )(base, index, queries, probs, grad_att, *spans)
    query_grad = (
        rotate(grad_q.reshape(LOCAL_HEADS, 2, HEAD_DIM // 2, ROWS), own_turn[0], -own_turn[1])
        .astype(BF)
        .reshape(GROUP, Q_PART, ROWS)
    )
    moved = jnp.concatenate([query_grad, attended.reshape(GROUP, Q_PART, ROWS)], axis=1)
    back_terms = scatter_terms(span_mine, span_theirs, "c", "x", index)
    moved = exchange(tie(moved, back_terms[0])).transpose(1, 0, 2).reshape(2 * Q_PART, 1024)
    query_grad, group_attended = moved[:Q_PART], moved[Q_PART:]
    back_terms[1] = tie(back_terms[1], moved)
    back = total_of(back_terms)
    back = (
        back[0]
        + push(back[1].astype(BF), "y", -1).astype(F32)
        + push(back[2].astype(BF), "y", -2).astype(F32)
    )
    grad_k = rotate(back[: 2 * PART].reshape(2, PART, 1024), group_turn[0], -group_turn[1])
    grad_v = back[2 * PART :].reshape(2, PART, 1024)
    pair_grad = jnp.concatenate([grad_k, grad_v]).astype(BF).reshape(KV_PART, 1024)

    sent = jnp.concatenate([query_grad, pair_grad])
    feed_grad = tie(feed_grad, sent)
    group_resid = lax.all_gather(tie(resid_low, feed_grad), ("x", "c"), axis=0)
    feed_grad = pair_total(feed_grad, 0, b, "b").astype(BF)
    side = jax.ShapeDtypeStruct((4, ROWS, D), BF)
    side_block = pl.BlockSpec((1, ROWS, D), lambda k: (k, 0, 0))
    norma_mine, norma_theirs, gain_a = pl.pallas_call(
        project_back,
        grid=(4,),
        out_shape=(side, side, jax.ShapeDtypeStruct((8, D), F32)),
        in_specs=[
            SMEM,
            pl.BlockSpec((Q_PART + KV_PART, 2 * ROWS), lambda k: (0, k)),
            small_block,
            token_block,
        ],
        out_specs=(side_block, side_block, gains_block),
        scratch_shapes=[pltpu.VMEM((2, ROWS, D), BF)],
        cost_estimate=SMALL,
        compiler_params=params(32),
    )(index, sent, w_small, group_tokens)
    rate_a = rms_rate(inflow)
    norma_terms = scatter_terms(norma_mine, norma_theirs, "c", "x", index, after=(feed_grad,))
    extra = jnp.concatenate([gain_a[:1], 0.5 * gain_b[None], jnp.zeros((6, D), F32)])
    parts = grads_by_chunk(
        normed_a, sent, extra, group_resid, group_attended, index, norma_terms[0]
    )
    row_terms = along_y(parts)
    norma_terms[1:] = [tie(term, *row_terms[1:]) for term in norma_terms[1:]]
    norma_low = low_bits(total_of(norma_terms))
    out_low = lax.psum_scatter(tie(feed_part, parts[0]), ("x", "c"), scatter_dimension=0)
    row_grad = pair_total(low_bits(total_of(row_terms)), 0, b, "b").astype(BF)
    late = jnp.concatenate([feed_grad, row_grad], axis=1)
    late = exchange(late.reshape(GROUP, OWNED, 3 * F_PAD + 512))
    small_grad = late[:, :, 3 * F_PAD : 3 * F_PAD + 256]
    other_out = swap(out_low, "t")
    out_tokens = (residual + (out_low.astype(F32) + other_out.astype(F32))).astype(BF)
    grad_norma = tensor_sum(norma_low)
    scaled = grad_norma * gains[0]
    input_grad = (
        grad_resid
        + rate_a * scaled
        - inflow * rate_a**3 * jnp.mean(scaled * inflow, axis=-1, keepdims=True)
    )


    def update(grads, weight, moment, second, part, start, rate, pair=False):
        return pl.pallas_call(
            adam_columns(part, start, rate, pair),
            out_shape=(jax.ShapeDtypeStruct(weight.shape, F32),) * 3,
            in_specs=[VMEM] * (3 + len(grads)),
            out_specs=(VMEM,) * 3,
            cost_estimate=SMALL,
            compiler_params=params(32),
        )(*grads, weight, moment, second)

    other_grad = swap(tie(small_grad, other_out), "t")
    query_new = update(
        [late], query_weight, query_moment, query_second, Q_PART, 3 * F_PAD, wide_rate
    )
    pair_new = update(
        [small_grad, other_grad],
        keyvalue_weight,
        keyvalue_moment,
        keyvalue_second,
        KV_PART,
        Q_PART,
        wide_rate,
        True,
    )
    output_new = update(
        [late], output_weight, output_moment, output_second, Q_PART, 3 * F_PAD + 256, output_rate
    )
    matrix = pl.BlockSpec((1, OWNED, 8 * F_PART), lambda k: (k, 0, 0))
    feed_new = pl.pallas_call(
        adam_columns(F_PART, 0, wide_rate),
        grid=(3,),
        out_shape=(jax.ShapeDtypeStruct(feedforward_weight.shape, F32),) * 3,
        in_specs=[pl.BlockSpec((GROUP, OWNED, F_PAD), lambda k: (0, 0, k))] + [matrix] * 3,
        out_specs=(matrix,) * 3,
        cost_estimate=SMALL,
        compiler_params=params(32),
    )(late, feedforward_weight, feedforward_moment, feedforward_second)
    gain_grad = small_grad.astype(F32) + other_grad.astype(F32)
    gain_grad = jnp.sum(gain_grad[:, :, Q_PART + KV_PART : Q_PART + KV_PART + 2], axis=0).T
    gains_new = adam(norm_gains, gain_grad, gains_moment, gains_second, 0.3, 0.0)
    return (
        out_tokens,
        input_grad,
        *query_new,
        *pair_new,
        *output_new,
        *feed_new,
        *gains_new,
    )


def solution(mesh):
    grid = Mesh(mesh.devices.reshape(2, 4, 4, 2, 2), ("b", "y", "x", "c", "t"))
    rows = ("b", "y", "x", "c")
    token = P(rows, None)
    split = P(rows, "t")
    whole = P(rows, None)
    feed = P(None, rows, "t")
    gain = P(None, rows)
    weights = (split,) * 3 + (whole,) * 3 + (split,) * 3 + (feed,) * 3 + (gain,) * 3
    return jax.shard_map(
        local,
        mesh=grid,
        in_specs=(token, token) + weights,
        out_specs=(token, token) + weights,
        check_vma=False,
    )
```

```python
import math

import jax
import jax.numpy as jnp
from jax import lax
from jax.experimental import pallas as pl
from jax.experimental.pallas import tpu as pltpu
from jax.sharding import Mesh
from jax.sharding import PartitionSpec as P

D = 2560
HEADS = 10
HEAD_DIM = 256
STEP = 10
ROWS = 128
GROUP = 8
OWNED = 40
Q_PART = 160
KV_PART = 64
F_PART = 480
F_PAD = 512
LOCAL_HEADS = 5
TILES = 17
BF = jnp.bfloat16
F32 = jnp.float32
ANY = pl.BlockSpec(memory_space=pl.ANY)
SMEM = pl.BlockSpec(memory_space=pltpu.SMEM)
VMEM = pl.BlockSpec(memory_space=pltpu.VMEM)


SMALL = pl.CostEstimate(flops=1, transcendentals=0, bytes_accessed=1)


def params(mib):
    return pltpu.CompilerParams(vmem_limit_bytes=mib * 1024 * 1024)


def dot(left, right, left_dim, right_dim):
    return lax.dot_general(
        left, right, (((left_dim,), (right_dim,)), ((), ())), preferred_element_type=F32
    )


def shift(value, axis, step):
    return lax.ppermute(value, axis, [(i, (i + step) % 4) for i in range(4)])


def push(value, axis, step):
    return lax.ppermute(value, axis, [(i, i + step) for i in range(4) if 0 <= i + step < 4])


def swap(value, axis):
    return lax.ppermute(value, axis, [(0, 1), (1, 0)])


STEPS = (0, 1, 3, 2)
Y_AT, X_AT, B_AT, C_AT = 0, 4, 8, 10


def tie(value, *others):
    def body(*refs):
        del refs

    return pl.pallas_call(
        body,
        out_shape=jax.ShapeDtypeStruct(value.shape, value.dtype),
        in_specs=[ANY] * (1 + len(others)),
        out_specs=ANY,
        input_output_aliases={0: 0},
        cost_estimate=SMALL,
    )(value, *others)


def place(pieces, index, shape, target):
    count = len(pieces)

    def body(index_ref, *refs):
        out, sems = refs[count], refs[count + 1]
        copies = [
            pltpu.make_async_copy(refs[k], target(out, index_ref, k), sems.at[k])
            for k in range(count)
        ]
        for copy in copies:
            copy.start()
        for copy in copies:
            copy.wait()

    return pl.pallas_call(
        body,
        out_shape=jax.ShapeDtypeStruct(shape, pieces[0].dtype),
        in_specs=[SMEM] + [VMEM] * count,
        out_specs=ANY,
        scratch_shapes=[pltpu.SemaphoreType.DMA((count,))],
        cost_estimate=SMALL,
        compiler_params=params(24),
    )(index, *pieces)


def direct(value, axis):
    return [value] + [shift(value, axis, step) for step in STEPS[1:]]


def group_place(mine, index):
    pieces = mine + [swap(piece, "c") for piece in mine]

    def target(out, index_ref, k):
        return out.at[2 * index_ref[X_AT + k % 4] + index_ref[C_AT + k // 4]]

    return place(pieces, index, (GROUP,) + mine[0].shape, target)


def group_gather(value, index):
    return group_place(direct(value, "x"), index)


def two_step_gather(value, index):
    half = value.shape[0] // 2
    left, right = shift(value, "x", 1), shift(value, "x", 3)
    top, bottom = shift(left[:half], "x", 1), shift(right[half:], "x", 3)
    mine = [value, left, right, top, bottom]
    pieces = mine + [swap(piece, "c") for piece in mine]
    pieces = [
        piece if k % 5 > 2 else piece.reshape((2, half) + value.shape[1:])
        for k, piece in enumerate(pieces)
    ]

    def target(out, index_ref, k):
        spot = 2 * index_ref[X_AT + min(k % 5, 3)] + index_ref[C_AT + k // 5]
        return out.at[spot] if k % 5 < 3 else out.at[spot, k % 5 - 3]

    out = place(pieces, index, (GROUP, 2, half) + value.shape[1:], target)
    return out.reshape((GROUP,) + value.shape), (left, right)


def place_rows(mine, index):
    pieces = mine + [swap(piece, "c") for piece in mine]

    def target(out, index_ref, k):
        spot = 2 * index_ref[X_AT + min(k % 5, 3)] + index_ref[C_AT + k // 5]
        if k % 5 < 3:
            return out.at[:, spot]
        return out.at[pl.ds((k % 5 - 3) * 4, 4), spot]

    width = mine[0].shape[2]
    return place(pieces, index, (8, GROUP, OWNED, width), target).reshape(D, width)


def pair_gather(mine, theirs, pair_axis, ring_axis, index, after=()):
    pieces = direct(jnp.stack([mine, theirs]), ring_axis)
    ring_at, pair_at = (X_AT, C_AT) if ring_axis == "x" else (Y_AT, B_AT)

    def body(index_ref, *refs):
        out, sems = refs[-2:]
        copies = []
        for k in range(4):
            for h in range(2):
                spot, side = index_ref[ring_at + k], index_ref[pair_at + h]
                to = out.at[spot, side] if ring_axis == "x" else out.at[side, spot]
                copies.append(pltpu.make_async_copy(refs[k].at[h], to, sems.at[2 * k + h]))
        for copy in copies:
            copy.start()
        for copy in copies:
            copy.wait()

    shape = ((4, 2) if ring_axis == "x" else (2, 4)) + mine.shape
    return pl.pallas_call(
        body,
        out_shape=jax.ShapeDtypeStruct(shape, mine.dtype),
        in_specs=[SMEM] + [VMEM] * 4 + [ANY] * len(after),
        out_specs=ANY,
        scratch_shapes=[pltpu.SemaphoreType.DMA((8,))],
        cost_estimate=SMALL,
        compiler_params=params(16),
    )(index, *pieces, *after)


def exchange_sends(mine, theirs, after=()):
    pair = jnp.stack([mine, swap(theirs, "c")], axis=1)
    if after:
        pair = tie(pair, *after)
    return [pair[0]] + [shift(pair[k], "x", STEPS[k]) for k in range(1, 4)]


def exchange_place(pieces, index):
    def body(index_ref, *refs):
        out, sems = refs[-2:]
        copies = []
        for k in range(4):
            for h in range(2):
                to = out.at[index_ref[X_AT + k], index_ref[C_AT + h]]
                copies.append(pltpu.make_async_copy(refs[k].at[h], to, sems.at[2 * k + h]))
        for copy in copies:
            copy.start()
        for copy in copies:
            copy.wait()

    return pl.pallas_call(
        body,
        out_shape=jax.ShapeDtypeStruct((4, 2) + pieces[0].shape[1:], pieces[0].dtype),
        in_specs=[SMEM] + [VMEM] * 4,
        out_specs=ANY,
        scratch_shapes=[pltpu.SemaphoreType.DMA((8,))],
        cost_estimate=SMALL,
        compiler_params=params(16),
    )(index, *pieces)


def group_exchange(mine, theirs, index):
    return exchange_place(exchange_sends(mine, theirs), index)


def fold(mine, received, index, at, after=()):
    shape = mine.shape[1:]

    def body(index_ref, mine_ref, received_ref, *refs):
        for k, out in enumerate(refs[len(after) :]):
            spot = index_ref[at + (0, 2, 1, 3)[k]]
            total = mine_ref[spot].astype(F32) + received_ref[spot].astype(F32)
            out[...] = total.astype(out.dtype)

    return pl.pallas_call(
        body,
        out_shape=(jax.ShapeDtypeStruct(shape, F32),) + (jax.ShapeDtypeStruct(shape, BF),) * 3,
        in_specs=[SMEM, VMEM, VMEM] + [ANY] * len(after),
        out_specs=(VMEM,) * 4,
        cost_estimate=SMALL,
        compiler_params=params(40),
    )(index, mine, received, *after)


def scatter_terms(mine, theirs, pair_axis, ring_axis, index, after=()):
    at = X_AT if ring_axis == "x" else Y_AT
    own, *others = fold(mine, swap(theirs, pair_axis), index, at, after)
    return [own] + [shift(other, ring_axis, step) for step, other in zip(STEPS[1:], others)]


def total_of(terms):
    return sum(term.astype(F32) for term in terms)


def scatter(*args, **kwargs):
    return total_of(scatter_terms(*args, **kwargs))


def pair_total(parts, axis, place_at, pair_axis):
    mine, theirs = sides(parts, axis, place_at)
    return mine.astype(F32) + swap(theirs, pair_axis).astype(F32)


def sides(parts, axis, place_at):
    return (
        lax.dynamic_index_in_dim(parts, place_at, axis, keepdims=False),
        lax.dynamic_index_in_dim(parts, 1 - place_at, axis, keepdims=False),
    )


def both_in_order(mine, theirs, place_at):
    first = place_at == 0
    return jnp.stack([jnp.where(first, mine, theirs), jnp.where(first, theirs, mine)])


def low_bits(value):
    return lax.optimization_barrier(value.astype(BF))


def tensor_sum(low):
    return low.astype(F32) + swap(low, "t").astype(F32)


def exchange(value):
    return lax.all_to_all(value, ("x", "c"), split_axis=0, concat_axis=0, tiled=True)


def hand_out(index_ref, held, mine_ref, theirs_ref):
    for k in range(4):
        spot = 2 * index_ref[X_AT + (0, 2, 1, 3)[k]]
        mine_ref[k] = held[spot + index_ref[C_AT]]
        theirs_ref[k] = held[spot + index_ref[C_AT + 1]]


def pack_small(index_ref, q_ref, kv_ref, gain_ref, mine_ref, theirs_ref, held):
    rest = jnp.zeros((OWNED, 256 - Q_PART - KV_PART - 2), F32)
    half, part = HEAD_DIM // 2, KV_PART // 4
    for j in range(GROUP):
        held[j] = jnp.concatenate(
            [
                q_ref[:, Q_PART * j : Q_PART * (j + 1)],
                kv_ref[:, part * j : part * (j + 1)],
                kv_ref[:, half + part * j : half + part * (j + 1)],
                kv_ref[:, 2 * half + 2 * part * j : 2 * half + 2 * part * (j + 1)],
                gain_ref[...],
                rest,
            ],
            axis=1,
        ).astype(BF)
    hand_out(index_ref, held, mine_ref, theirs_ref)


def pack_feed(index_ref, w_ref, after_ref, mine_ref, theirs_ref, held):
    del after_ref
    rest = jnp.zeros((OWNED, F_PAD - F_PART), F32)
    for j in range(GROUP):
        held[j] = jnp.concatenate(
            [w_ref[0, :, F_PART * j : F_PART * (j + 1)], rest], axis=1
        ).astype(BF)
    hand_out(index_ref, held, mine_ref, theirs_ref)


def adam(weight, grad, moment, second, rate, decay):
    moment_new = 0.9 * moment + 0.1 * grad
    second_new = 0.95 * second + 0.05 * grad * grad
    ratio = moment_new / (1.0 - 0.9**STEP) / (jnp.sqrt(second_new / (1.0 - 0.95**STEP)) + 1e-08)
    return (moment_new, second_new, weight - rate * (ratio + decay * weight))


def adam_columns(part, start, rate, pair=False):
    if pair:
        cuts = [(start, PART), (start + PART, PART), (start + 2 * PART, 2 * PART)]
    else:
        cuts = [(start, part)]

    def body(*refs):
        *g_refs, w_ref, m_ref, v_ref, mo_ref, vo_ref, wo_ref = refs
        grad = sum(
            jnp.concatenate(
                [
                    g_ref[j, :, at : at + count].astype(F32)
                    for at, count in cuts
                    for j in range(GROUP)
                ],
                axis=1,
            )
            for g_ref in g_refs
        )
        index = (0,) if len(w_ref.shape) == 3 else (slice(None),)
        m, v, w = adam(w_ref[index], grad, m_ref[index], v_ref[index], rate, 0.1)
        mo_ref[index] = m
        vo_ref[index] = v
        wo_ref[index] = w

    return body


def window(base_ref, i):
    start = pl.multiple_of(ROWS * (base_ref[1] + i), ROWS)
    return pl.ds(start, ROWS), base_ref[0] * 8 + base_ref[1] + i >= 16


PART = HEAD_DIM // 16


def head_rows(j):
    return (
        (slice(2 * PART * j, 2 * PART * j + PART), slice(PART * j, PART * j + PART)),
        (
            slice(2 * PART * j + PART, 2 * PART * (j + 1)),
            slice(HEAD_DIM // 2 + PART * j, HEAD_DIM // 2 + PART * (j + 1)),
        ),
    )


def hold_spans(index_ref, pieces, keys, values):
    for k, piece in enumerate(pieces):
        spot = 2 * index_ref[X_AT + k % 4] + index_ref[C_AT + k // 4]
        rows = pl.ds(pl.multiple_of(2 * PART * spot, 2 * PART), 2 * PART)
        for back in range(3):
            lanes = slice(1024 * (2 - back), 1024 * (3 - back))
            keys[rows, lanes] = piece[back, : 2 * PART]
            values[rows, lanes] = piece[back, 2 * PART :]


def hold_queries(q_ref, qs):
    for h in range(LOCAL_HEADS):
        for j in range(GROUP):
            for to, at in head_rows(j):
                qs[to, ROWS * h : ROWS * (h + 1)] = q_ref[h, at]


def attend(base_ref, index_ref, q_ref, *refs):
    pieces, (p_ref, a_ref, qs, keys, values) = refs[:GROUP], refs[GROUP:]
    hold_spans(index_ref, pieces, keys, values)
    hold_queries(q_ref, qs)
    width = LOCAL_HEADS * ROWS
    key_at = lax.broadcasted_iota(jnp.int32, (ROWS, width), 0)
    query_at = lax.broadcasted_iota(jnp.int32, (ROWS, width), 1) % ROWS
    top = jnp.full((1, width), -1e30, F32)
    for i in range(TILES):
        lanes, exists = window(base_ref, i)
        scores = dot(keys[:, lanes], qs[...], 0, 0) * (HEAD_DIM**-0.5)
        if i == 0:
            scores = jnp.where((key_at > query_at) & exists, scores, -1e30)
        elif i == TILES - 1:
            scores = jnp.where(key_at <= query_at, scores, -1e30)
        else:
            scores = jnp.where(exists, scores, -1e30)
        p_ref[i] = scores
        top = jnp.maximum(top, jnp.max(scores, axis=0, keepdims=True))
    total = jnp.zeros((1, width), F32)
    for i in range(TILES):
        weights = jnp.exp(p_ref[i] - top)
        p_ref[i] = weights
        total = total + jnp.sum(weights, axis=0, keepdims=True)
    scale = 1.0 / total
    result = jnp.zeros((HEAD_DIM, width), F32)
    for i in range(TILES):
        lanes, _ = window(base_ref, i)
        probs = p_ref[i] * scale
        p_ref[i] = probs
        result = result + dot(values[:, lanes], probs.astype(BF), 1, 0)
    for h in range(LOCAL_HEADS):
        a_ref[h] = result[:, ROWS * h : ROWS * (h + 1)].astype(BF)


def attend_back(base_ref, index_ref, q_ref, p_ref, da_ref, *refs):
    pieces = refs[:GROUP]
    dq_ref, mine_ref, theirs_ref, qs, das, dps, keys, values, d_keys, d_values = refs[-10:]
    hold_spans(index_ref, pieces, keys, values)
    hold_queries(q_ref, qs)
    width = LOCAL_HEADS * ROWS
    for h in range(LOCAL_HEADS):
        das[:, ROWS * h : ROWS * (h + 1)] = da_ref[h]
    d_keys[...] = jnp.zeros(d_keys.shape, BF)
    d_values[...] = jnp.zeros(d_values.shape, BF)
    delta = jnp.zeros((1, width), F32)
    for i in range(TILES):
        lanes, _ = window(base_ref, i)
        probs = p_ref[i]
        d_probs = dot(values[:, lanes], das[...], 0, 0)
        dps[i] = d_probs
        delta = delta + jnp.sum(probs * d_probs, axis=0, keepdims=True)
        d_values[:, lanes] = dot(das[...], probs.astype(BF), 1, 1).astype(BF)
    dq = jnp.zeros((HEAD_DIM, width), F32)
    for i in range(TILES):
        lanes, _ = window(base_ref, i)
        d_scores = (p_ref[i] * (dps[i] - delta)).astype(BF)
        dq = dq + dot(keys[:, lanes], d_scores, 1, 0)
        d_keys[:, lanes] = (dot(qs[...], d_scores, 1, 1) * (HEAD_DIM**-0.5)).astype(BF)
    for h in range(LOCAL_HEADS):
        for j in range(GROUP):
            for at, to in head_rows(j):
                dq_ref[h, to] = dq[at, ROWS * h : ROWS * (h + 1)] * (HEAD_DIM**-0.5)
    core = base_ref[1] % 2
    for j in range(GROUP):
        rows = slice(2 * PART * j, 2 * PART * (j + 1))
        for ref, match in ((mine_ref, j % 2), (theirs_ref, 1 - j % 2)):

            @pl.when(core == match)
            def _(ref=ref, rows=rows, j=j):
                for back in range(3):
                    lanes = slice(1024 * (2 - back), 1024 * (3 - back))
                    ref[j // 2, back, : 2 * PART] = d_keys[rows, lanes]
                    ref[j // 2, back, 2 * PART :] = d_values[rows, lanes]


def project(x_ref, w_ref, n_ref, raw_ref, gains_ref):
    @pl.when(pl.program_id(0) == 0)
    def _():
        turned = w_ref[:, 128:].astype(F32).T
        at = Q_PART + KV_PART - 128
        gains_ref[...] = turned[at : at + 8]

    x = x_ref[...].reshape(2 * ROWS, D).astype(F32)
    normed = (x * rms_rate(x) * gains_ref[0:1]).astype(BF)
    n_ref[...] = normed.reshape(2, ROWS, D)
    raw_ref[...] = dot(normed, w_ref[...], 1, 0).T


def project_back(index_ref, sent_ref, w_ref, x_ref, mine_ref, theirs_ref, gain_ref, held):
    @pl.when(pl.program_id(0) == 0)
    def _():
        gain_ref[...] = jnp.zeros(gain_ref.shape, F32)

    sent = sent_ref[...].astype(F32).T.astype(BF)
    part = dot(sent, w_ref[:, : Q_PART + KV_PART], 1, 1)
    x = x_ref[...].reshape(2 * ROWS, D).astype(F32)
    gain_ref[0:1] += jnp.sum(part * x * rms_rate(x), axis=0, keepdims=True)
    held[...] = part.astype(BF).reshape(2, ROWS, D)
    mine_ref[0] = held[index_ref[C_AT]]
    theirs_ref[0] = held[index_ref[C_AT + 1]]


def chunk_grads(index_ref, rows_ref, cols_ref, extra_ref, rows2_ref, cols2_ref, after_ref, *refs):
    del after_ref
    *out_refs, total, held = refs
    step, part, part2 = pl.program_id(0), cols_ref.shape[0], cols2_ref.shape[0]

    @pl.when(step == 0)
    def _():
        total[...] = jnp.zeros(total.shape, F32)
        total[part : part + 8] = extra_ref[...]

    @pl.when(step < 4)
    def _():
        total[:part] += dot(cols_ref[...], rows_ref[...].reshape(2 * ROWS, D), 1, 0)

    @pl.when(step >= 4)
    def _():
        rows = rows2_ref[...].reshape(2 * ROWS, D)
        total[256 : 256 + part2] += dot(cols2_ref[...], rows, 1, 0)

    @pl.when(step == 7)
    def _():
        block, whole = GROUP * OWNED, total[...].T
        for k in range(8):
            held[k % 4, k // 4] = whole[k * block : (k + 1) * block].astype(BF)
        for k, out in enumerate(out_refs):
            out[...] = held[index_ref[Y_AT + (0, 2, 1, 3)[k]]]


def grads_by_chunk(rows, cols, extra, rows2, cols2, index, after):
    shape = (2, GROUP * OWNED, 512)

    def first(k):
        return jnp.minimum(k, 3)

    def second(k):
        return jnp.maximum(k - 4, 0)

    return pl.pallas_call(
        chunk_grads,
        grid=(8,),
        out_shape=(jax.ShapeDtypeStruct(shape, BF),) * 4,
        in_specs=[
            SMEM,
            pl.BlockSpec((2, ROWS, D), lambda k: (first(k), 0, 0)),
            pl.BlockSpec((cols.shape[0], 2 * ROWS), lambda k: (0, first(k))),
            pl.BlockSpec((8, D), lambda k: (0, 0)),
            pl.BlockSpec((2, ROWS, D), lambda k: (second(k), 0, 0)),
            pl.BlockSpec((cols2.shape[0], 2 * ROWS), lambda k: (0, second(k))),
            ANY,
        ],
        out_specs=(pl.BlockSpec(shape, lambda k: (0, 0, 0)),) * 4,
        scratch_shapes=[
            pltpu.VMEM((512, D), F32),
            pltpu.VMEM((4, 2, GROUP * OWNED, 512), BF),
        ],
        cost_estimate=SMALL,
        compiler_params=params(40),
    )(index, rows, cols, extra, rows2, cols2, after)


def along_y(parts):
    return [parts[0]] + [shift(part, "y", step) for step, part in zip(STEPS[1:], parts[1:])]


def rms_rate(values):
    return lax.rsqrt(jnp.mean(values * values, axis=-1, keepdims=True) + 1e-06)


def rotate(values, cosine, sine):
    first, second = values[..., 0, :, :], values[..., 1, :, :]
    return jnp.stack([first * cosine - second * sine, second * cosine + first * sine], axis=-3)


def local(
    tokens,
    cotangent,
    query_weight,
    query_moment,
    query_second,
    keyvalue_weight,
    keyvalue_moment,
    keyvalue_second,
    output_weight,
    output_moment,
    output_second,
    feedforward_weight,
    feedforward_moment,
    feedforward_second,
    norm_gains,
    gains_moment,
    gains_second,
):
    x, y, c, b = (lax.axis_index(name) for name in "xycb")
    j = 2 * x + c
    wide_rate = 1.5 * D**-0.5
    output_rate = 1.5 * (HEADS * HEAD_DIM // 32) ** -0.5
    index = jnp.stack(
        [(y + 4 - step) % 4 for step in STEPS] + [(x + 4 - step) % 4 for step in STEPS]
        + [b, 1 - b, c, 1 - c]
    ).astype(jnp.int32)
    base = jnp.stack([y, j]).astype(jnp.int32)

    inflow = tokens.astype(F32)
    parcel = jax.ShapeDtypeStruct((4, OWNED, 256), BF)
    parcels = pl.pallas_call(
        pack_small,
        out_shape=(parcel, parcel),
        in_specs=[SMEM] + [VMEM] * 3,
        out_specs=(VMEM, VMEM),
        scratch_shapes=[pltpu.VMEM((GROUP, OWNED, 256), BF)],
        cost_estimate=SMALL,
        compiler_params=params(16),
    )(index, query_weight, keyvalue_weight, norm_gains.T)
    small = group_exchange(*parcels, index).reshape(GROUP * OWNED, 256)
    group_tokens = lax.all_gather(tie(tokens, small), ("x", "c"), axis=0)
    partner = swap(small, "b")
    w_small = pair_gather(small, partner, "b", "y", index).reshape(D, 256)
    rows = tie(output_weight.astype(BF), w_small)
    rows = pair_gather(rows, swap(rows, "b"), "b", "y", index).reshape(8, OWNED, -1)
    parcel = jax.ShapeDtypeStruct((4, OWNED, 3 * F_PAD), BF)
    parcel_block = pl.BlockSpec((4, OWNED, F_PAD), lambda k: (0, 0, k))
    parcels = pl.pallas_call(
        pack_feed,
        grid=(3,),
        out_shape=(parcel, parcel),
        in_specs=[SMEM, pl.BlockSpec((1, OWNED, 8 * F_PART), lambda k: (k, 0, 0)), ANY],
        out_specs=(parcel_block, parcel_block),
        scratch_shapes=[pltpu.VMEM((GROUP, OWNED, F_PAD), BF)],
        cost_estimate=SMALL,
        compiler_params=params(24),
    )(index, feedforward_weight, partner)
    feed = exchange_sends(*parcels, (group_tokens, rows))
    feed = exchange_place(feed, index).reshape(GROUP * OWNED, 3 * F_PAD)
    feed_partner = swap(feed, "b")
    w_small = tie(w_small, feed)
    rows = tie(rows, group_tokens)
    rows_left, rows_right = shift(rows, "x", 1), shift(rows, "x", 3)

    token_block = pl.BlockSpec((2, ROWS, D), lambda k: (k, 0, 0))
    small_block = pl.BlockSpec((D, 256), lambda k: (0, 0))
    gains_block = pl.BlockSpec((8, D), lambda k: (0, 0))
    normed_a, raw, gains = pl.pallas_call(
        project,
        grid=(4,),
        out_shape=(
            jax.ShapeDtypeStruct((GROUP, ROWS, D), BF),
            jax.ShapeDtypeStruct((256, 1024), F32),
            jax.ShapeDtypeStruct((8, D), F32),
        ),
        in_specs=[token_block, small_block],
        out_specs=(token_block, pl.BlockSpec((256, 2 * ROWS), lambda k: (0, k)), gains_block),
        cost_estimate=SMALL,
        compiler_params=params(32),
    )(group_tokens, w_small)
    steps = jnp.arange(HEAD_DIM // 2, dtype=F32)
    freqs = jnp.exp(steps * (-2.0 * math.log(10000.0) / HEAD_DIM))
    first = y * 1024

    def turn(frequencies, first, count):
        places = (first + jnp.arange(count, dtype=jnp.int32)).astype(F32)
        angle = frequencies[:, None] * places[None, :]
        return jnp.cos(angle), jnp.sin(angle)

    group_turn = turn(lax.dynamic_slice_in_dim(freqs, PART * j, PART), first, 1024)
    own_turn = turn(freqs, first + ROWS * j, ROWS)
    keys = rotate(raw[Q_PART : Q_PART + 2 * PART].reshape(2, PART, 1024), *group_turn)
    values = raw[Q_PART + 2 * PART : Q_PART + KV_PART].reshape(2, PART, 1024)
    pair = jnp.concatenate([keys, values]).astype(BF).reshape(KV_PART, 1024)
    pair = tie(pair, rows_left, rows_right)
    rows_top, rows_bottom = shift(rows_left[:4], "x", 1), shift(rows_right[4:], "x", 3)
    pair_back = [push(pair, "y", 1), push(pair, "y", 2)]
    q_raw = raw[:Q_PART].astype(BF).reshape(Q_PART, GROUP, ROWS).transpose(1, 0, 2)
    q_raw = exchange(q_raw)
    feed_partner = tie(feed_partner, *pair_back)
    q_raw = q_raw.astype(F32).reshape(LOCAL_HEADS, 2, HEAD_DIM // 2, ROWS)
    queries = rotate(q_raw, *own_turn).astype(BF).reshape(LOCAL_HEADS, HEAD_DIM, ROWS)
    spans = direct(jnp.stack([pair] + pair_back), "x")
    spans[1:] = [tie(span, q_raw, rows_top, rows_bottom) for span in spans[1:]]
    feed_pair = both_in_order(feed, feed_partner, b)
    w_feed = lax.all_gather(feed_pair, "y", axis=1, tiled=True).reshape(D, 3 * F_PAD)
    back_pieces = direct(tie(cotangent, *spans[1:]), "x")
    spans = spans + [swap(piece, "c") for piece in spans]
    rows_top = tie(rows_top, *spans[5:])
    w_output = place_rows([rows, rows_left, rows_right, rows_top, rows_bottom], index)

    width = LOCAL_HEADS * ROWS
    held_spans = [pltpu.VMEM((HEAD_DIM, 3072), BF)] * 2
    probs, attended = pl.pallas_call(
        attend,
        out_shape=(
            jax.ShapeDtypeStruct((TILES, ROWS, width), F32),
            jax.ShapeDtypeStruct((LOCAL_HEADS, HEAD_DIM, ROWS), BF),
        ),
        in_specs=[SMEM, SMEM] + [VMEM] * 9,
        out_specs=(VMEM, VMEM),
        scratch_shapes=[pltpu.VMEM((HEAD_DIM, width), BF)] + held_spans,
        cost_estimate=SMALL,
        compiler_params=params(40),
    )(base, index, queries, *spans)
    attended = attended.reshape(LOCAL_HEADS * HEAD_DIM, ROWS)
    branch = low_bits(dot(attended, w_output, 0, 1))
    back_pieces[1:] = [tie(piece, branch) for piece in back_pieces[1:]]
    other_branch = tie(swap(branch, "t"), *back_pieces[1:])
    residual = inflow + (branch.astype(F32) + other_branch.astype(F32))

    rate_b = rms_rate(residual)
    normed_b = tie((residual * rate_b * gains[1]).astype(BF), w_feed)
    group_b = lax.all_gather(normed_b, ("x", "c"), axis=0).reshape(1024, D)
    group_back = group_place(back_pieces, index).reshape(1024, D)
    d_hidden = tie(dot(group_back, w_feed[:, 2 * F_PAD :], 1, 0), normed_b)
    gate_up = dot(group_b, w_feed[:, : 2 * F_PAD], 1, 0)
    gate, up = gate_up[:, :F_PAD], gate_up[:, F_PAD:]
    root = math.sqrt(2.0 / math.pi)
    bend = jnp.tanh(root * (gate + 0.044715 * gate * gate * gate))
    gelu = 0.5 * gate * (1.0 + bend)
    slope = 0.5 * (1.0 + bend) + 0.5 * gate * (1.0 - bend * bend) * root * (
        1.0 + 3.0 * 0.044715 * gate * gate
    )
    hidden = (gelu * up).astype(BF)
    d_gate_up = jnp.concatenate(
        [(d_hidden * up * slope).astype(BF), (d_hidden * gelu).astype(BF)], axis=1
    )
    normb_part = low_bits(dot(d_gate_up, w_feed[:, : 2 * F_PAD], 1, 1))
    normb_low = lax.psum_scatter(
        normb_part.reshape(GROUP, ROWS, D), ("x", "c"), scatter_dimension=0
    )
    down_grad = dot(tie(group_back, normb_part), hidden, 0, 0).astype(BF)
    gate_grad = dot(tie(group_b, normb_part), d_gate_up, 0, 0).astype(BF)
    feed_part = low_bits(dot(hidden, w_feed[:, 2 * F_PAD :], 1, 1)).reshape(GROUP, ROWS, D)
    normb_low = tie(normb_low, down_grad, gate_grad, feed_part)
    grad_normb = tensor_sum(normb_low)
    feed_grad = jnp.concatenate([gate_grad, down_grad], axis=1).reshape(2, -1, 3 * F_PAD)
    feed_grad = lax.psum_scatter(feed_grad, "y", scatter_dimension=1, tiled=True)
    scaled = grad_normb * gains[1]
    grad_resid = (
        cotangent.astype(F32)
        + rate_b * scaled
        - residual * rate_b**3 * jnp.mean(scaled * residual, axis=-1, keepdims=True)
    )
    gain_b = jnp.sum(grad_normb * residual * rate_b, axis=0)
    resid_low = grad_resid.astype(BF)
    grad_att = dot(w_output, resid_low, 0, 1).astype(BF).reshape(LOCAL_HEADS, HEAD_DIM, ROWS)

    span_parts = jax.ShapeDtypeStruct((4, 3, KV_PART, 1024), BF)
    grad_q, span_mine, span_theirs = pl.pallas_call(
        attend_back,
        out_shape=(
            jax.ShapeDtypeStruct((LOCAL_HEADS, HEAD_DIM, ROWS), F32),
            span_parts,
            span_parts,
        ),
        in_specs=[SMEM, SMEM] + [VMEM] * 11,
        out_specs=(VMEM, VMEM, VMEM),
        scratch_shapes=[
            pltpu.VMEM((HEAD_DIM, width), BF),
            pltpu.VMEM((HEAD_DIM, width), BF),
            pltpu.VMEM((TILES, ROWS, width), F32),
        ]
        + held_spans * 2,
        cost_estimate=SMALL,
        compiler_params=params(44),
    )(base, index, queries, probs, grad_att, *spans)
    query_grad = (
        rotate(grad_q.reshape(LOCAL_HEADS, 2, HEAD_DIM // 2, ROWS), own_turn[0], -own_turn[1])
        .astype(BF)
        .reshape(GROUP, Q_PART, ROWS)
    )
    moved = jnp.concatenate([query_grad, attended.reshape(GROUP, Q_PART, ROWS)], axis=1)
    back_terms = scatter_terms(span_mine, span_theirs, "c", "x", index)
    moved = exchange(tie(moved, back_terms[0])).transpose(1, 0, 2).reshape(2 * Q_PART, 1024)
    query_grad, group_attended = moved[:Q_PART], moved[Q_PART:]
    back_terms[1] = tie(back_terms[1], moved)
    back = total_of(back_terms)
    back = (
        back[0]
        + push(back[1].astype(BF), "y", -1).astype(F32)
        + push(back[2].astype(BF), "y", -2).astype(F32)
    )
    grad_k = rotate(back[: 2 * PART].reshape(2, PART, 1024), group_turn[0], -group_turn[1])
    grad_v = back[2 * PART :].reshape(2, PART, 1024)
    pair_grad = jnp.concatenate([grad_k, grad_v]).astype(BF).reshape(KV_PART, 1024)

    sent = jnp.concatenate([query_grad, pair_grad])
    feed_grad = tie(feed_grad, sent)
    group_resid = lax.all_gather(tie(resid_low, feed_grad), ("x", "c"), axis=0)
    feed_grad = pair_total(feed_grad, 0, b, "b").astype(BF)
    side = jax.ShapeDtypeStruct((4, ROWS, D), BF)
    side_block = pl.BlockSpec((1, ROWS, D), lambda k: (k, 0, 0))
    norma_mine, norma_theirs, gain_a = pl.pallas_call(
        project_back,
        grid=(4,),
        out_shape=(side, side, jax.ShapeDtypeStruct((8, D), F32)),
        in_specs=[
            SMEM,
            pl.BlockSpec((Q_PART + KV_PART, 2 * ROWS), lambda k: (0, k)),
            small_block,
            token_block,
        ],
        out_specs=(side_block, side_block, gains_block),
        scratch_shapes=[pltpu.VMEM((2, ROWS, D), BF)],
        cost_estimate=SMALL,
        compiler_params=params(32),
    )(index, sent, w_small, group_tokens)
    rate_a = rms_rate(inflow)
    norma_terms = scatter_terms(norma_mine, norma_theirs, "c", "x", index)
    norma_terms[0] = tie(norma_terms[0], feed_grad)
    extra = jnp.concatenate([gain_a[:1], 0.5 * gain_b[None], jnp.zeros((6, D), F32)])
    parts = grads_by_chunk(
        normed_a, sent, extra, group_resid, group_attended, index, norma_terms[0]
    )
    row_terms = along_y(parts)
    norma_terms[1:] = [tie(term, *row_terms[1:]) for term in norma_terms[1:]]
    norma_low = low_bits(total_of(norma_terms))
    out_low = lax.psum_scatter(tie(feed_part, parts[0]), ("x", "c"), scatter_dimension=0)
    row_grad = pair_total(low_bits(total_of(row_terms)), 0, b, "b").astype(BF)
    late = jnp.concatenate([feed_grad, row_grad], axis=1)
    late = exchange(late.reshape(GROUP, OWNED, 3 * F_PAD + 512))
    small_grad = late[:, :, 3 * F_PAD : 3 * F_PAD + 256]
    other_out = swap(out_low, "t")
    out_tokens = (residual + (out_low.astype(F32) + other_out.astype(F32))).astype(BF)
    grad_norma = tensor_sum(norma_low)
    scaled = grad_norma * gains[0]
    input_grad = (
        grad_resid
        + rate_a * scaled
        - inflow * rate_a**3 * jnp.mean(scaled * inflow, axis=-1, keepdims=True)
    )


    def update(grads, weight, moment, second, part, start, rate, pair=False):
        return pl.pallas_call(
            adam_columns(part, start, rate, pair),
            out_shape=(jax.ShapeDtypeStruct(weight.shape, F32),) * 3,
            in_specs=[VMEM] * (3 + len(grads)),
            out_specs=(VMEM,) * 3,
            cost_estimate=SMALL,
            compiler_params=params(32),
        )(*grads, weight, moment, second)

    other_grad = swap(tie(small_grad, other_out), "t")
    query_new = update(
        [late], query_weight, query_moment, query_second, Q_PART, 3 * F_PAD, wide_rate
    )
    pair_new = update(
        [small_grad, other_grad],
        keyvalue_weight,
        keyvalue_moment,
        keyvalue_second,
        KV_PART,
        Q_PART,
        wide_rate,
        True,
    )
    output_new = update(
        [late], output_weight, output_moment, output_second, Q_PART, 3 * F_PAD + 256, output_rate
    )
    matrix = pl.BlockSpec((1, OWNED, 8 * F_PART), lambda k: (k, 0, 0))
    feed_new = pl.pallas_call(
        adam_columns(F_PART, 0, wide_rate),
        grid=(3,),
        out_shape=(jax.ShapeDtypeStruct(feedforward_weight.shape, F32),) * 3,
        in_specs=[pl.BlockSpec((GROUP, OWNED, F_PAD), lambda k: (0, 0, k))] + [matrix] * 3,
        out_specs=(matrix,) * 3,
        cost_estimate=SMALL,
        compiler_params=params(32),
    )(late, feedforward_weight, feedforward_moment, feedforward_second)
    gain_grad = small_grad.astype(F32) + other_grad.astype(F32)
    gain_grad = jnp.sum(gain_grad[:, :, Q_PART + KV_PART : Q_PART + KV_PART + 2], axis=0).T
    gains_new = adam(norm_gains, gain_grad, gains_moment, gains_second, 0.3, 0.0)
    return (
        out_tokens,
        input_grad,
        *query_new,
        *pair_new,
        *output_new,
        *feed_new,
        *gains_new,
    )


def solution(mesh):
    grid = Mesh(mesh.devices.reshape(2, 4, 4, 2, 2), ("b", "y", "x", "c", "t"))
    rows = ("b", "y", "x", "c")
    token = P(rows, None)
    split = P(rows, "t")
    whole = P(rows, None)
    feed = P(None, rows, "t")
    gain = P(None, rows)
    weights = (split,) * 3 + (whole,) * 3 + (split,) * 3 + (feed,) * 3 + (gain,) * 3
    return jax.shard_map(
        local,
        mesh=grid,
        in_specs=(token, token) + weights,
        out_specs=(token, token) + weights,
        check_vma=False,
    )
```
